128 devices in a mesh: sa: 8 (over x_lo, y), sb: 16 (over z, x_hi, core).
Axes of the slice: x: 4 (x_hi: 2, x_lo: 2; x = x_hi * 2 + x_lo), y: 4, z: 4, core: 2. Of those that a mesh axis runs over, the one named last changes fastest.
Arguments:
- gate_signal: bfloat16 [8192, 4096], P(('sa', 'sb')), may hold values from -6 to 6
- key_signal: bfloat16 [8192, 4096], P(('sa', 'sb')), may hold values from -6 to 6
- value_signal: bfloat16 [8192, 4096], P(('sa', 'sb')), may hold values from -6 to 6
- long_filter: bfloat16 [8192, 4096], P(('sa', 'sb')), may hold values from -2 to 2
- skip_gain: float32 [4096], replicated, may hold values from 0.5 to 1.5
- head_weight: bfloat16 [4096, 32, 384], P(None, 'sb'), may hold values from -0.5 to 0.5
Outputs:
- mixed: bfloat16 [8192, 4096], P(('sa', 'sb'))
- attended: bfloat16 [8192, 4096], P(('sa', 'sb'))
The draws below stay inside these ranges and needn't reach their ends.
All inputs are finite; a program needn't handle non-finite values.
Results may differ from the reference program's by a relative error of at most 0.025.
The reference program's roundings to bfloat16 on the way (of `product` and `filtered`) count: a program that leaves them out, or rounds other values in their place, can miss the bound.
Values may be sent and summed in bfloat16 or wider, within the bound.
No kernel may reach another device: no remote copies, remote signals or barrier semaphores. Data moves between devices by JAX's collectives and lax.ppermute only.
A program may use at most 192 MiB of HBM per device.

```python
import jax
import jax.numpy as jnp
from jax import lax

CONV_CHANNELS = 4096
HD = 128
HEADS = 32
SEQUENCE_LENGTH = 8192


def draw_long_filter(key, part):
    key = jax.random.fold_in(key, 11)
    keys_all = jax.random.split(key, 9)
    step_count = jnp.arange(SEQUENCE_LENGTH, dtype=jnp.float32)[:, None]
    slow_share = 0.5
    slow_rate = jnp.exp(jax.random.uniform(keys_all[0], (1, CONV_CHANNELS), minval=jnp.log(0.3 / SEQUENCE_LENGTH), maxval=jnp.log(2.3 / SEQUENCE_LENGTH)))
    fast_rate = jnp.exp(jax.random.uniform(keys_all[1], (1, CONV_CHANNELS), minval=jnp.log(1.0 / 400.0), maxval=jnp.log(1.0 / 30.0)))
    is_slow = jax.random.uniform(keys_all[2], (1, CONV_CHANNELS)) < slow_share
    decay_rate = jnp.where(is_slow, slow_rate, fast_rate)
    spike_amplitude = jnp.ones((SEQUENCE_LENGTH, CONV_CHANNELS), jnp.float32)
    for turn in range(3):
        location_index = jax.random.randint(keys_all[3 + turn], (1, CONV_CHANNELS), 1, SEQUENCE_LENGTH).astype(jnp.float32)
        multiplier = jax.random.uniform(keys_all[6], (1, CONV_CHANNELS), minval=0.5, maxval=0.8)
        keys_all = keys_all.at[6].set(jax.random.fold_in(keys_all[6], turn + 1))
        spike_amplitude = spike_amplitude * jnp.where(step_count >= location_index, multiplier, 1.0)
    scale_amount = jnp.sqrt((1.0 - jnp.exp(-2.0 * decay_rate)) / (1.0 - jnp.exp(-2.0 * decay_rate * SEQUENCE_LENGTH)))
    random_jitter = jnp.clip(jax.random.normal(keys_all[7], (SEQUENCE_LENGTH, CONV_CHANNELS), jnp.float32), -6.0, 6.0)
    return (random_jitter * jnp.exp(-decay_rate * step_count) * spike_amplitude * scale_amount).astype(jnp.bfloat16)


def draw_head_weight(key, part):
    key = jax.random.fold_in(key, 23)
    first = jax.random.fold_in(key, 0)
    base = jnp.clip(jax.random.normal(first, (CONV_CHANNELS, HEADS, 3 * HD), jnp.float32), -6.0, 6.0) * CONV_CHANNELS ** (-0.5)
    weight = base
    return jnp.clip(weight, -0.5, 0.5).astype(jnp.bfloat16)


def levels(own_key, shape, pieces, low, largest):
    factor_of, own = 1.0, jax.random.fold_in(own_key, 6)
    for position, parts in pieces:
        heights = jnp.exp(jax.random.uniform(jax.random.fold_in(own, position), (parts,), jnp.float32, low / len(pieces), largest / len(pieces)))
        factor_of = factor_of * jnp.repeat(heights, shape[position] // parts).reshape([-1 if axis == position else 1 for axis in range(len(shape))])
    return factor_of


def normal_values(key, dims, spread, bound, shards=(), kind=jnp.bfloat16):
    values = jax.random.normal(key, dims, jnp.float32) * spread
    if len(shards) > 0:
        values = levels(key, dims, shards, -0.22, 0.18) * values
    return jnp.clip(values, min=-bound, max=bound).astype(kind)


def setup_inputs(seed: int = 0) -> dict:
    arg_keys = jax.random.split(jax.random.key(seed), 7)
    return {
        "gate_signal": normal_values(arg_keys[0], (SEQUENCE_LENGTH, CONV_CHANNELS), 1.0, 6.0, ((0, 128),)),
        "key_signal": normal_values(arg_keys[1], (SEQUENCE_LENGTH, CONV_CHANNELS), 1.0, 6.0, ((0, 128),)),
        "value_signal": normal_values(arg_keys[2], (SEQUENCE_LENGTH, CONV_CHANNELS), 1.0, 6.0, ((0, 128),)),
        "long_filter": draw_long_filter(jax.random.fold_in(arg_keys[6], 71), 0),
        "skip_gain": jnp.clip(jax.random.uniform(arg_keys[4], (CONV_CHANNELS,), jnp.float32, 0.5, 1.5), 0.5, 1.5),
        "head_weight": draw_head_weight(jax.random.fold_in(arg_keys[6], 71), 0),
    }


def convolve_block(pair):
    signal, taps = pair
    length = signal.shape[0]
    spectrum = jnp.fft.rfft(signal, n=2 * length, axis=0) * jnp.fft.rfft(taps, n=2 * length, axis=0)
    return jnp.fft.irfft(spectrum, n=2 * length, axis=0)[:length]

def reference(gate_signal, key_signal, value_signal, long_filter, skip_gain, head_weight):
    product = (key_signal.astype(jnp.float32) * value_signal.astype(jnp.float32)).astype(jnp.bfloat16)
    signal = product.astype(jnp.float32)
    taps = long_filter.astype(jnp.float32)
    width = min(256, CONV_CHANNELS)
    signal_blocks = signal.reshape(SEQUENCE_LENGTH, CONV_CHANNELS // width, width).transpose(1, 0, 2)
    tap_blocks = taps.reshape(SEQUENCE_LENGTH, CONV_CHANNELS // width, width).transpose(1, 0, 2)
    conv = lax.map(convolve_block, (signal_blocks, tap_blocks)).transpose(1, 0, 2).reshape(SEQUENCE_LENGTH, CONV_CHANNELS)
    filtered = lax.optimization_barrier((conv + skip_gain[None, :] * signal).astype(jnp.bfloat16))
    mixed = (gate_signal.astype(jnp.float32) * filtered.astype(jnp.float32)).astype(jnp.bfloat16)
    block = min(512, SEQUENCE_LENGTH)
    key_pos = jnp.arange(SEQUENCE_LENGTH, dtype=jnp.int32)
    weight_heads = jnp.transpose(head_weight, (1, 0, 2))

    def one_head(head_w):
        projected = jnp.dot(mixed, head_w, preferred_element_type=jnp.float32)
        queries = projected[:, :HD].astype(jnp.bfloat16)
        keys = projected[:, HD:2 * HD].astype(jnp.bfloat16)
        values = projected[:, 2 * HD:].astype(jnp.bfloat16).astype(jnp.float32)
        query_blocks = queries.reshape(SEQUENCE_LENGTH // block, block, HD)

        def attend(item):
            query_block, index = item
            query_pos = index * block + jnp.arange(block, dtype=jnp.int32)
            scores = jnp.dot(query_block, keys.T, preferred_element_type=jnp.float32) * (1.0 / jnp.sqrt(jnp.float32(HD)))
            allowed = key_pos[None, :] <= query_pos[:, None]
            masked = jnp.where(allowed, scores, jnp.float32(-1e+30))
            highest = lax.optimization_barrier(jnp.max(masked, axis=1, keepdims=True))
            weights = jnp.where(allowed, jnp.exp(masked - highest), jnp.float32(0.0))
            probs = weights / lax.optimization_barrier(jnp.sum(weights, axis=1, keepdims=True))
            return jnp.dot(probs, values, precision=lax.Precision.HIGHEST)
        indices = jnp.arange(SEQUENCE_LENGTH // block, dtype=jnp.int32)
        return lax.map(attend, (query_blocks, indices)).reshape(SEQUENCE_LENGTH, HD)
    outputs = lax.map(one_head, weight_heads)
    attended = jnp.transpose(outputs, (1, 0, 2)).reshape(SEQUENCE_LENGTH, HEADS * HD).astype(jnp.bfloat16)
    return (mixed, attended)
```

```python
import itertools
import math

import jax
import jax.numpy as jnp
import ml_dtypes
import numpy as np
from jax import lax
from jax.experimental import pallas as pl
from jax.experimental.pallas import tpu as pltpu
from jax.sharding import Mesh, PartitionSpec as P

BF = jnp.bfloat16
F32 = jnp.float32
NAMES = ("xl", "yh", "yl", "z", "xh", "c")
SIZES = (2, 2, 2, 4, 2, 2)
ROWS = 64
DEVS = 128
SEQ = ROWS * DEVS
CHANS = 4096
HALF = CHANS // 2
HD = 128
VMEM_LIMIT = 56 * 1024 * 1024


def split16(table):
    table = np.asarray(table, np.float64)
    high = table.astype(np.float32).astype(ml_dtypes.bfloat16)
    low = (table - high.astype(np.float64)).astype(np.float32).astype(ml_dtypes.bfloat16)
    return high, low


def conv_tables():
    d = np.arange(DEVS)
    k1 = np.arange(DEVS) + 0.25
    r = np.arange(ROWS)
    outer = 2 * math.pi * np.outer(k1, d) / DEVS
    first = np.concatenate([np.cos(outer), -np.sin(outer)], axis=0)
    twist = 2 * math.pi * np.outer(k1, r) / SEQ
    twist_cos = np.tile(np.cos(twist), (1, 2)).astype(np.float32)
    twist_sin = np.tile(np.sin(twist), (1, 2)).astype(np.float32)
    inner = 2 * math.pi * np.outer(r, r) / ROWS
    eye = np.eye(2)
    cos, sin = np.kron(eye, np.cos(inner)), np.kron(eye, np.sin(inner))
    second = np.block([[cos, -sin], [sin, cos]])
    third = np.block([[cos, sin], [-sin, cos]])
    last = np.concatenate([np.cos(outer).T, -np.sin(outer).T], axis=1) / SEQ
    return (*split16(first), twist_cos, twist_sin, *split16(second), *split16(third), *split16(last))


def whole(shape):
    return pl.BlockSpec(shape, lambda *_: (0,) * len(shape), memory_space=pltpu.VMEM)


def params(**more):
    return pltpu.CompilerParams(vmem_limit_bytes=VMEM_LIMIT, **more)


def pack_kernel(key_ref, value_ref, taps_ref, out_ref):
    def both(ref, start):
        return jnp.concatenate(
            [ref[:, pl.ds(start, 128)].astype(F32), ref[:, pl.ds(start + HALF, 128)].astype(F32)], axis=0
        )

    for block in range(HALF // 128):
        start = block * 128
        product = (both(key_ref, start) * both(value_ref, start)).astype(BF).astype(F32)
        for which, tile in enumerate((product, both(taps_ref, start))):
            out_ref[block * 8 : block * 8 + 8, which] = tile.T.astype(BF).reshape(8, 16, 128)


def pack(key_signal, value_signal, long_filter):
    return pl.pallas_call(
        pack_kernel,
        out_shape=jax.ShapeDtypeStruct((DEVS, 2, 16, 128), BF),
        in_specs=[whole((ROWS, CHANS))] * 3,
        out_specs=whole((DEVS, 2, 16, 128)),
        compiler_params=params(),
        name="pack",
    )(key_signal, value_signal, long_filter)


def dot(a, b):
    return jnp.dot(a, b, preferred_element_type=F32)


def cut(x):
    high = x.astype(BF)
    return high, (x - high.astype(F32)).astype(BF)


def conv_kernel(
    recv_ref, gain_ref, w1h, w1l, tc_ref, ts_ref, m2h, m2l, m3h, m3l, w3h, w3l, out_ref, x_s, h_s, y_s
):
    x_s[...] = recv_ref[:, 0].astype(F32).reshape(DEVS * 16, 128)
    h_s[...] = recv_ref[:, 1].astype(F32).reshape(DEVS * 16, 128)
    tc = tc_ref[...]
    ts = ts_ref[...]

    def three(a, bh, bl):
        ah, al = cut(a)
        return dot(ah, bh) + (dot(al, bh) + dot(ah, bl))

    def step(it, carry):
        rows = [pl.ds(it * 2 + u, DEVS, stride=16) for u in range(2)]
        xs = [x_s[row, :] for row in rows]
        hs = [h_s[row, :] for row in rows]
        signal = jnp.concatenate([v.astype(BF) for v in xs + hs], axis=1)
        first = dot(w1h[...], signal) + dot(w1l[...], signal)
        stacked = []
        for u in range(4):
            re = first[:DEVS, u * 128 : u * 128 + 128]
            im = first[DEVS:, u * 128 : u * 128 + 128]
            stacked.append(jnp.concatenate([re * tc + im * ts, im * tc - re * ts], axis=1))
        spectrum = three(jnp.concatenate(stacked, axis=0), m2h[...], m2l[...])
        prods = []
        for u in range(2):
            s = spectrum[u * 128 : u * 128 + 128]
            h = spectrum[256 + u * 128 : 256 + u * 128 + 128]
            sr, si, hr, hi = s[:, :128], s[:, 128:], h[:, :128], h[:, 128:]
            prods.append(jnp.concatenate([sr * hr - si * hi, sr * hi + si * hr], axis=1))
        back = three(jnp.concatenate(prods, axis=0), m3h[...], m3l[...])
        outs = []
        for u in range(2):
            re = back[u * 128 : u * 128 + 128, :128]
            im = back[u * 128 : u * 128 + 128, 128:]
            outs.append(jnp.concatenate([re * tc - im * ts, im * tc + re * ts], axis=0))
        vh, vl = cut(jnp.concatenate(outs, axis=1))
        conv = dot(w3h[...], vh) + (dot(w3l[...], vh) + dot(w3h[...], vl))
        for u in range(2):
            gain = gain_ref[pl.ds(it * 2 + u, 1), :]
            y_s[rows[u], :] = conv[:, u * 128 : u * 128 + 128] + gain * xs[u]
        return carry

    lax.fori_loop(0, 8, step, 0)
    out_ref[...] = y_s[...].reshape(DEVS, 16, 128).astype(BF)


def convolve(recv, gain):
    tables = conv_tables()
    args = (recv, gain, *[jnp.asarray(t) for t in tables])
    return pl.pallas_call(
        conv_kernel,
        out_shape=jax.ShapeDtypeStruct((DEVS, 16, 128), BF),
        in_specs=[whole(a.shape) for a in args],
        out_specs=whole((DEVS, 16, 128)),
        scratch_shapes=[pltpu.VMEM((DEVS * 16, 128), F32)] * 3,
        compiler_params=params(),
        name="convolve",
    )(*args)


def gate_kernel(recv_ref, gate_ref, out_ref):
    for block in range(HALF // 128):
        tile = recv_ref[block * 8 : block * 8 + 8].astype(F32).reshape(128, 128).T
        for half in range(2):
            cols = pl.ds(half * HALF + block * 128, 128)
            part = tile[half * ROWS : half * ROWS + ROWS]
            out_ref[:, cols] = (gate_ref[:, cols].astype(F32) * part).astype(BF)


def apply_gate(recv, gate_signal):
    return pl.pallas_call(
        gate_kernel,
        out_shape=jax.ShapeDtypeStruct((ROWS, CHANS), BF),
        in_specs=[whole((DEVS, 16, 128)), whole((ROWS, CHANS))],
        out_specs=whole((ROWS, CHANS)),
        compiler_params=params(),
        name="apply_gate",
    )(recv, gate_signal)


def project_kernel(place_ref, *refs):
    shards = refs[:8]
    w_ref, out_ref, x_s, sems = refs[8:]

    @pl.when(pl.program_id(0) == 0)
    def _():
        copies = [
            pltpu.make_async_copy(shard, x_s.at[pl.ds(i * ROWS, ROWS), :], sems.at[i])
            for i, shard in enumerate(shards)
        ]
        for copy in copies:
            copy.start()
        for copy in copies:
            copy.wait()

    result = dot(x_s[...], w_ref[0])
    for slot, part in enumerate((1, 2, 0)):
        out_ref[0, slot] = result[:, part * HD : part * HD + HD].astype(BF)


def project(place, shards, weights):
    rows = 8 * ROWS
    return pl.pallas_call(
        project_kernel,
        out_shape=jax.ShapeDtypeStruct((4, 3, rows, HD), BF),
        grid_spec=pltpu.PrefetchScalarGridSpec(
            num_scalar_prefetch=1,
            grid=(4,),
            in_specs=[pl.BlockSpec(memory_space=pl.ANY)] * 8
            + [pl.BlockSpec((1, CHANS, 3 * HD), lambda i, place: (i // 2, 0, i % 2))],
            out_specs=pl.BlockSpec((1, 3, rows, HD), lambda i, place: (place[i], 0, 0, 0)),
            scratch_shapes=[pltpu.VMEM((rows, CHANS), BF), pltpu.SemaphoreType.DMA((8,))],
        ),
        compiler_params=params(),
        name="project",
    )(place, *shards, weights)


GROUP = 8 * ROWS
TILE = 256
SCALE = math.log2(math.e) / math.sqrt(HD)
EXTRA = 16


def attend_kernel(me_ref, q_ref, own_ref, sib_ref, out_ref, vt_s):
    me, my_z, my_xh, my_c = me_ref[0], me_ref[1], me_ref[2], me_ref[3]
    ones = jnp.ones((EXTRA, GROUP), BF)
    for side, ref in enumerate((own_ref, sib_ref)):
        for rel in range(8):
            vt_s[side, rel, :HD] = ref[rel, 1].astype(F32).T.astype(BF)
            vt_s[side, rel, HD:] = ones

    def inner_pos(index, core):
        z = (my_z + (index >> 7)) & 3
        xh = my_xh ^ ((index >> 6) & 1)
        return z * 256 + xh * 128 + core * 64 + (index & 63)

    row = lax.broadcasted_iota(jnp.int32, (GROUP, TILE), 0)
    col = lax.broadcasted_iota(jnp.int32, (GROUP, TILE), 1)

    for qrel in range(4):
        group = me ^ (qrel * 2)
        queries = [q_ref[qrel, t * TILE : t * TILE + TILE] for t in range(2)]

        def visit(rel, carry, masked):
            done = []
            for t in range(2):
                best, acc = carry[t]
                scores = []
                for side, ref in enumerate((own_ref, sib_ref)):
                    s = lax.dot_general(
                        ref[rel, 0], queries[t], (((1,), (1,)), ((), ())), preferred_element_type=F32
                    )
                    if masked:
                        key_pos = inner_pos(row, my_c ^ side)
                        query_pos = inner_pos(col + t * TILE, my_c)
                        s = jnp.where(key_pos <= query_pos, s, -1e30)
                    scores.append(s)
                top = jnp.maximum(
                    jnp.max(scores[0], axis=0, keepdims=True), jnp.max(scores[1], axis=0, keepdims=True)
                )
                new = jnp.maximum(best, top)
                shrink = jnp.exp2((best - new) * SCALE)
                acc = acc * shrink
                for side in range(2):
                    weight = jnp.exp2((scores[side] - new) * SCALE).astype(BF)
                    acc = acc + dot(vt_s[side, rel], weight)
                done.append((new, acc))
            return tuple(done)

        start = tuple(
            (jnp.full((1, TILE), -1e30, F32), jnp.zeros((HD + EXTRA, TILE), F32)) for _ in range(2)
        )
        carry = visit(qrel * 2, start, True)
        carry = lax.fori_loop(0, group, lambda g, cr: visit(g ^ me, cr, False), carry)
        for t in range(2):
            acc = carry[t][1]
            out = (acc[:HD] / acc[HD : HD + 1]).T.astype(BF)
            for part in range(TILE // ROWS):
                shard = t * (TILE // ROWS) + part
                z = (my_z + (shard >> 1)) & 3
                xh = my_xh ^ (shard & 1)
                out_ref[(group >> 1) * 8 + z * 2 + xh] = out[part * ROWS : part * ROWS + ROWS]


def attend(place, queries, own, sib):
    return pl.pallas_call(
        attend_kernel,
        out_shape=jax.ShapeDtypeStruct((32, ROWS, HD), BF),
        in_specs=[pl.BlockSpec(memory_space=pltpu.SMEM)]
        + [whole((4, GROUP, HD)), whole((8, 2, GROUP, HD)), whole((8, 2, GROUP, HD))],
        out_specs=whole((32, ROWS, HD)),
        scratch_shapes=[pltpu.VMEM((2, 8, HD + EXTRA, GROUP), BF)],
        compiler_params=params(),
        name="attend",
    )(place, queries, own, sib)


def shift(x, move):
    pairs = []
    for spot in itertools.product(*[range(n) for n in SIZES]):
        target = dict(zip(NAMES, spot))
        move(target)
        goal = [target[n] % size for n, size in zip(NAMES, SIZES)]
        pairs.append((int(np.ravel_multi_index(spot, SIZES)), int(np.ravel_multi_index(goal, SIZES))))
    return lax.ppermute(x, NAMES, pairs)


def along_z(x, step):
    def move(t):
        t["z"] = (t["z"] + step) % 4

    return shift(x, move)


def flip(x, **bits):
    def move(t):
        for name, bit in bits.items():
            t[name] ^= bit

    return shift(x, move)


def per_device(gate_signal, key_signal, value_signal, long_filter, skip_gain, head_weight):
    at = {name: lax.axis_index(name) for name in NAMES}
    device = lax.axis_index(NAMES)

    packed = pack(key_signal, value_signal, long_filter)
    recv = lax.all_to_all(packed, NAMES, split_axis=0, concat_axis=0, tiled=True)

    own_weight = head_weight.reshape(CHANS, 6 * HD)
    weights = jnp.stack([own_weight, flip(own_weight, c=1)])

    gain = lax.dynamic_slice_in_dim(skip_gain.reshape(2, HALF), device * 16, 16, 1)
    gain = jnp.repeat(gain.T, ROWS, axis=1)
    filtered = convolve(recv, gain)
    returned = lax.all_to_all(filtered, NAMES, split_axis=0, concat_axis=0, tiled=True)
    mixed = apply_gate(returned, gate_signal)

    from_z = [mixed, along_z(mixed, -1), along_z(mixed, -2), along_z(mixed, -3)]
    shards = []
    for part in from_z:
        shards += [part, flip(part, xh=1)]

    places = []
    for side in range(2):
        for i in range(2):
            places.append((at["xl"] ^ at["c"] ^ side) * 2 + (at["yh"] ^ i))
    projected = project(jnp.stack(places).astype(jnp.int32), shards, weights)

    kv, queries = [], []
    for rel in range(8):
        xl, yh, yl = rel >> 2, (rel >> 1) & 1, rel & 1
        part = projected[rel >> 1]
        part = part if yl == 0 else part[:2]
        got = part if rel == 0 else flip(part, xl=xl, yh=yh, yl=yl)
        kv.append(got[:2])
        if yl == 0:
            queries.append(got[2])
    own = jnp.stack(kv)
    sib = flip(own, c=1)
    group = at["xl"] * 4 + at["yh"] * 2 + at["yl"]
    place = jnp.stack([group, at["z"], at["xh"], at["c"]]).astype(jnp.int32)
    heads = attend(place, jnp.stack(queries), own, sib)

    out = lax.all_to_all(heads, ("xl", "yh", "z", "xh"), split_axis=0, concat_axis=0, tiled=True)
    out = out.reshape(2, 2, 4, 2, ROWS, HD).transpose(4, 2, 3, 0, 1, 5)
    return mixed, out.reshape(ROWS, CHANS)


def solution(mesh):
    fine = Mesh(mesh.devices.reshape(SIZES), NAMES)
    rows = P(NAMES, None)
    return jax.shard_map(
        per_device,
        mesh=fine,
        in_specs=(rows, rows, rows, rows, P(), P(None, ("z", "xh", "c"), None)),
        out_specs=(rows, rows),
        check_vma=False,
    )
```

```python
import functools
import itertools
import math

import jax
import jax.numpy as jnp
import ml_dtypes
import numpy as np
from jax import lax
from jax.experimental import pallas as pl
from jax.experimental.pallas import tpu as pltpu
from jax.sharding import Mesh, PartitionSpec as P

BF = jnp.bfloat16
F32 = jnp.float32
NAMES = ("xl", "yh", "yl", "z", "xh", "c")
SIZES = (2, 2, 2, 4, 2, 2)
ROWS = 64
DEVS = 128
SEQ = ROWS * DEVS
CHANS = 4096
HALF = CHANS // 2
HD = 128
VMEM_LIMIT = 56 * 1024 * 1024


def split16(table):
    table = np.asarray(table, np.float64)
    high = table.astype(np.float32).astype(ml_dtypes.bfloat16)
    low = (table - high.astype(np.float64)).astype(np.float32).astype(ml_dtypes.bfloat16)
    return high, low


def conv_tables():
    d = np.arange(DEVS)
    k1 = np.arange(DEVS) + 0.25
    r = np.arange(ROWS)
    outer = 2 * math.pi * np.outer(k1, d) / DEVS
    first = np.concatenate([np.cos(outer), -np.sin(outer)], axis=0)
    twist = 2 * math.pi * np.outer(k1, r) / SEQ
    twist_cos = np.tile(np.cos(twist), (1, 2)).astype(np.float32)
    twist_sin = np.tile(np.sin(twist), (1, 2)).astype(np.float32)
    inner = 2 * math.pi * np.outer(r, r) / ROWS
    eye = np.eye(2)
    cos, sin = np.kron(eye, np.cos(inner)), np.kron(eye, np.sin(inner))
    second = np.block([[cos, -sin], [sin, cos]])
    third = np.block([[cos, sin], [-sin, cos]])
    last = np.concatenate([np.cos(outer).T, -np.sin(outer).T], axis=1) / SEQ
    return (*split16(first), twist_cos, twist_sin, *split16(second), *split16(third), *split16(last))


def whole(shape):
    return pl.BlockSpec(shape, lambda *_: (0,) * len(shape), memory_space=pltpu.VMEM)


def params(**more):
    return pltpu.CompilerParams(vmem_limit_bytes=VMEM_LIMIT, **more)


def pack_kernel(key_ref, value_ref, taps_ref, out_ref):
    def both(ref, start):
        return jnp.concatenate(
            [ref[:, pl.ds(start, 128)].astype(F32), ref[:, pl.ds(start + HALF, 128)].astype(F32)], axis=0
        )

    for block in range(HALF // 128):
        start = block * 128
        product = (both(key_ref, start) * both(value_ref, start)).astype(BF).astype(F32)
        for which, tile in enumerate((product, both(taps_ref, start))):
            out_ref[block * 8 : block * 8 + 8, which] = tile.T.astype(BF).reshape(8, 16, 128)


def pack(key_signal, value_signal, long_filter):
    return pl.pallas_call(
        pack_kernel,
        out_shape=jax.ShapeDtypeStruct((DEVS, 2, 16, 128), BF),
        in_specs=[whole((ROWS, CHANS))] * 3,
        out_specs=whole((DEVS, 2, 16, 128)),
        compiler_params=params(),
        name="pack",
    )(key_signal, value_signal, long_filter)


def dot(a, b):
    return jnp.dot(a, b, preferred_element_type=F32)


def cut(x):
    high = x.astype(BF)
    return high, (x - high.astype(F32)).astype(BF)


def conv_kernel(
    recv_ref, gain_ref, w1h, w1l, tc_ref, ts_ref, m2h, m2l, m3h, m3l, w3h, w3l, out_ref, x_s, h_s, y_s
):
    x_s[...] = recv_ref[:, 0].astype(F32).reshape(DEVS * 16, 128)
    h_s[...] = recv_ref[:, 1].astype(F32).reshape(DEVS * 16, 128)
    tc = tc_ref[...]
    ts = ts_ref[...]

    def three(a, bh, bl):
        ah, al = cut(a)
        return dot(ah, bh) + (dot(al, bh) + dot(ah, bl))

    def step(it, carry):
        rows = [pl.ds(it * 2 + u, DEVS, stride=16) for u in range(2)]
        xs = [x_s[row, :] for row in rows]
        hs = [h_s[row, :] for row in rows]
        signal = jnp.concatenate([v.astype(BF) for v in xs + hs], axis=1)
        first = dot(w1h[...], signal) + dot(w1l[...], signal)
        stacked = []
        for u in range(4):
            re = first[:DEVS, u * 128 : u * 128 + 128]
            im = first[DEVS:, u * 128 : u * 128 + 128]
            stacked.append(jnp.concatenate([re * tc + im * ts, im * tc - re * ts], axis=1))
        spectrum = three(jnp.concatenate(stacked, axis=0), m2h[...], m2l[...])
        prods = []
        for u in range(2):
            s = spectrum[u * 128 : u * 128 + 128]
            h = spectrum[256 + u * 128 : 256 + u * 128 + 128]
            sr, si, hr, hi = s[:, :128], s[:, 128:], h[:, :128], h[:, 128:]
            prods.append(jnp.concatenate([sr * hr - si * hi, sr * hi + si * hr], axis=1))
        back = three(jnp.concatenate(prods, axis=0), m3h[...], m3l[...])
        outs = []
        for u in range(2):
            re = back[u * 128 : u * 128 + 128, :128]
            im = back[u * 128 : u * 128 + 128, 128:]
            outs.append(jnp.concatenate([re * tc - im * ts, im * tc + re * ts], axis=0))
        vh, vl = cut(jnp.concatenate(outs, axis=1))
        conv = dot(w3h[...], vh) + (dot(w3l[...], vh) + dot(w3h[...], vl))
        for u in range(2):
            gain = gain_ref[pl.ds(it * 2 + u, 1), :]
            y_s[rows[u], :] = conv[:, u * 128 : u * 128 + 128] + gain * xs[u]
        return carry

    lax.fori_loop(0, 8, step, 0)
    out_ref[...] = y_s[...].reshape(DEVS, 16, 128).astype(BF)


def convolve(recv, gain):
    tables = conv_tables()
    args = (recv, gain, *[jnp.asarray(t) for t in tables])
    return pl.pallas_call(
        conv_kernel,
        out_shape=jax.ShapeDtypeStruct((DEVS, 16, 128), BF),
        in_specs=[whole(a.shape) for a in args],
        out_specs=whole((DEVS, 16, 128)),
        scratch_shapes=[pltpu.VMEM((DEVS * 16, 128), F32)] * 3,
        compiler_params=params(),
        name="convolve",
    )(*args)


PART = ROWS // 2


def gate_kernel(recv_ref, gate_ref, out_ref, upper_ref, lower_ref):
    for block in range(HALF // 128):
        tile = recv_ref[block * 8 : block * 8 + 8].astype(F32).reshape(128, 128).T
        for half in range(2):
            cols = pl.ds(half * HALF + block * 128, 128)
            part = tile[half * ROWS : half * ROWS + ROWS]
            mixed = (gate_ref[:, cols].astype(F32) * part).astype(BF)
            out_ref[:, cols] = mixed
            upper_ref[:, cols] = mixed[:PART]
            lower_ref[:, cols] = mixed[PART:]


def apply_gate(recv, gate_signal):
    shapes = [(ROWS, CHANS), (PART, CHANS), (PART, CHANS)]
    return pl.pallas_call(
        gate_kernel,
        out_shape=[jax.ShapeDtypeStruct(shape, BF) for shape in shapes],
        in_specs=[whole((DEVS, 16, 128)), whole((ROWS, CHANS))],
        out_specs=[whole(shape) for shape in shapes],
        compiler_params=params(),
        name="apply_gate",
    )(recv, gate_signal)


BLOCK = 8 * PART
ASKED = BLOCK // 2
MESSAGE = 2 * BLOCK + ASKED
DEPTH = 1024


def project_kernel(core_ref, *refs):
    shards = refs[:16]
    weights = refs[16:18]
    out_ref, acc = refs[18:]
    step = pl.program_id(0)
    x = jnp.concatenate([shard[...] for shard in shards], axis=0)

    for side in range(2):
        part = dot(x, weights[side][...])

        @pl.when(step == 0)
        def _():
            acc[side] = part

        @pl.when(step > 0)
        def _():
            acc[side] += part

    @pl.when(step == pl.num_programs(0) - 1)
    def _():
        for xl in range(2):
            for yh in range(2):
                start = yh * 3 * HD
                side = core_ref[0] ^ xl
                queries = acc[side, :, start : start + HD].astype(BF).reshape(2, 8, 2, PART // 2, HD)
                keys = acc[side, :, start + HD : start + 2 * HD].astype(BF)
                values = acc[side, :, start + 2 * HD : start + 3 * HD]
                flipped = [values[n * HD : n * HD + HD].T.astype(BF) for n in range(2 * BLOCK // HD)]
                for yl in range(2):
                    goal = xl * 4 + yh * 2 + yl
                    for part in range(2):
                        out_ref[goal, part, :BLOCK] = keys[part * BLOCK : part * BLOCK + BLOCK]
                        for n in range(BLOCK // HD):
                            first = BLOCK + n * HD
                            out_ref[goal, part, first : first + HD] = flipped[part * (BLOCK // HD) + n]
                        out_ref[goal, part, 2 * BLOCK :] = queries[part, :, yl].reshape(ASKED, HD)


def project(core, shards, own, sib, depth=DEPTH):
    return pl.pallas_call(
        project_kernel,
        out_shape=jax.ShapeDtypeStruct((8, 2, MESSAGE, HD), BF),
        grid_spec=pltpu.PrefetchScalarGridSpec(
            num_scalar_prefetch=1,
            grid=(CHANS // depth,),
            in_specs=[pl.BlockSpec((PART, depth), lambda i, core: (0, i))] * 16
            + [pl.BlockSpec((depth, 6 * HD), lambda i, core: (i, 0))] * 2,
            out_specs=whole((8, 2, MESSAGE, HD)),
            scratch_shapes=[pltpu.VMEM((2, 2 * BLOCK, 6 * HD), F32)],
        ),
        cost_estimate=pl.CostEstimate(
            flops=4 * BLOCK * CHANS * 12 * HD, bytes_accessed=CHANS * 12 * HD * 2, transcendentals=0
        ),
        compiler_params=params(),
        name="project",
    )(core, *shards, own, sib)


SCALE = math.log2(math.e) / math.sqrt(HD)
EXTRA = 16
KEYS = 4 * BLOCK
QUERIES = 2 * ASKED


PAIR = 2 * QUERIES
ROOM = 80.0
REACH = 170.0


def attend_kernel(me_ref, *refs):
    own_hbm, sib_hbm, out_ref, k_s, v_s, q_s, acc_s, sems = refs
    my_yl, my_z, my_xh, my_c = me_ref[0], me_ref[1], me_ref[2], me_ref[3]

    def fetch(group):
        copies = []

        def add(source, target):
            copies.append(pltpu.make_async_copy(source, target, sems.at[group, len(copies)]))

        for n in range(4):
            source = (own_hbm, sib_hbm)[n // 2].at[:, n % 2]
            add(source.at[group, pl.ds(0, BLOCK)], k_s.at[group, pl.ds(n * BLOCK, BLOCK)])
            for tile in range(BLOCK // HD):
                add(
                    source.at[group, pl.ds(BLOCK + tile * HD, HD)],
                    v_s.at[group, pl.ds(0, HD), pl.ds(n * BLOCK + tile * HD, HD)],
                )
            if n < 2:
                add(source.at[group, pl.ds(2 * BLOCK, ASKED)], q_s.at[group, pl.ds(n * ASKED, ASKED)])
        return copies

    for group in range(8):
        for copy in fetch(group):
            copy.start()
    for group in range(8):
        v_s[group, HD:] = jnp.ones((EXTRA, KEYS), BF)

    def inner_pos(shard, core, r):
        return ((my_z + (shard >> 1)) & 3) * 256 + (my_xh ^ (shard & 1)) * 128 + core * ROWS + r

    row = lax.broadcasted_iota(jnp.int32, (KEYS, 1), 0)
    col = lax.broadcasted_iota(jnp.int32, (1, PAIR), 1)
    key_pos = inner_pos((row >> 5) & 7, my_c ^ (row >> 9), ((row >> 8) & 1) * PART + (row & 31))
    query_pos = inner_pos(
        (col >> 4) & 7, my_c, ((col >> 7) & 1) * PART + my_yl * (PART // 2) + (col & 15)
    ) + (col >> 8) * 1024

    def nt(a, b):
        return lax.dot_general(a, b, (((1,), (1,)), ((), ())), preferred_element_type=F32)

    def score(group, queries, which):
        s = nt(k_s[group], queries)
        if which is not None:
            s = jnp.where(key_pos + which * 1024 <= query_pos, s, -1e30)
        return s

    def pair(k, tallest):
        groups = (2 * k, 2 * k + 1)
        for group in groups:
            for copy in fetch(group):
                copy.wait()
        queries = jnp.concatenate([q_s[group] for group in groups], axis=0)
        itself = jnp.concatenate(
            [
                k_s[group, pl.ds(pl.multiple_of(part * BLOCK + shard * PART + my_yl * 16, 16), 16)]
                for group in groups
                for part in range(2)
                for shard in range(8)
            ],
            axis=0,
        )
        ones = jnp.ones((16, HD), BF)
        for group in groups:
            square = nt(ones, jnp.square(k_s[group].astype(F32)).astype(BF))
            tallest = jnp.maximum(tallest, jnp.max(square[:8], axis=1, keepdims=True))
        size = nt(ones, jnp.square(queries.astype(F32)).astype(BF))[:1]
        bound = jnp.sqrt(size * tallest[:1]) * (SCALE * 1.02)
        product = (queries.astype(F32) * itself.astype(F32)).astype(BF)
        own = nt(ones, product)[:1] * SCALE
        safe = jnp.max(bound * 1.01 - own) <= REACH
        acc_s[...] = jnp.zeros(acc_s.shape, F32)

        @pl.when(safe)
        def _():
            offset = bound - ROOM

            def visit(group, which=None):
                weight = jnp.exp2(score(group, queries, which) * SCALE - offset).astype(BF)
                acc_s[...] += dot(v_s[group], weight)

            visit(groups[0], 0)
            visit(groups[1], 1)

            @pl.loop(0, 2 * k)
            def _(group):
                visit(group)

        @pl.when(jnp.logical_not(safe))
        def _():
            def visit(group, best, which=None):
                s = score(group, queries, which)
                new = jnp.maximum(best, jnp.max(s, axis=0, keepdims=True))
                weight = jnp.exp2((s - new) * SCALE).astype(BF)
                acc_s[...] = acc_s[...] * jnp.exp2((best - new) * SCALE) + dot(v_s[group], weight)
                return new

            best = visit(groups[0], jnp.full((1, PAIR), -1e30, F32), 0)
            best = visit(groups[1], best, 1)
            lax.fori_loop(0, 2 * k, visit, best)

        out = (acc_s[:HD] / acc_s[HD : HD + 1]).T.astype(BF)
        for n, group in enumerate(groups):
            for shard in range(8):
                z = (my_z + (shard >> 1)) & 3
                xh = my_xh ^ (shard & 1)
                for part in range(2):
                    first = n * QUERIES + part * ASKED + shard * 16
                    out_ref[group * 8 + z * 2 + xh, part * 16 : part * 16 + 16] = out[first : first + 16]
        return tallest

    lax.fori_loop(0, 4, pair, jnp.zeros((8, 1), F32))


def attend(place, own, sib):
    return pl.pallas_call(
        attend_kernel,
        out_shape=jax.ShapeDtypeStruct((64, PART, HD), BF),
        in_specs=[pl.BlockSpec(memory_space=pltpu.SMEM)] + [pl.BlockSpec(memory_space=pl.ANY)] * 2,
        out_specs=whole((64, PART, HD)),
        scratch_shapes=[
            pltpu.VMEM((8, KEYS, HD), BF),
            pltpu.VMEM((8, HD + EXTRA, KEYS), BF),
            pltpu.VMEM((8, QUERIES, HD), BF),
            pltpu.VMEM((HD + EXTRA, PAIR), F32),
            pltpu.SemaphoreType.DMA((8, 14)),
        ],
        compiler_params=params(),
        name="attend",
    )(place, own, sib)


def shift(x, move):
    pairs = []
    for spot in itertools.product(*[range(n) for n in SIZES]):
        target = dict(zip(NAMES, spot))
        move(target)
        goal = [target[n] % size for n, size in zip(NAMES, SIZES)]
        pairs.append((int(np.ravel_multi_index(spot, SIZES)), int(np.ravel_multi_index(goal, SIZES))))
    return lax.ppermute(x, NAMES, pairs)


def along_z(x, step):
    def move(t):
        t["z"] = (t["z"] + step) % 4

    return shift(x, move)


def flip(x, **bits):
    def move(t):
        for name, bit in bits.items():
            t[name] ^= bit

    return shift(x, move)


def per_device(gate_signal, key_signal, value_signal, long_filter, skip_gain, head_weight):
    at = {name: lax.axis_index(name) for name in NAMES}
    device = lax.axis_index(NAMES)

    packed = pack(key_signal, value_signal, long_filter)
    recv = lax.all_to_all(packed, NAMES, split_axis=0, concat_axis=0, tiled=True)

    own_weight = head_weight.reshape(CHANS, 6 * HD)
    sib_weight = flip(head_weight, c=1).reshape(CHANS, 6 * HD)

    gain = lax.dynamic_slice_in_dim(skip_gain.reshape(2, HALF), device * 16, 16, 1)
    gain = jnp.repeat(gain.T, ROWS, axis=1)
    recv, own_weight, sib_weight = lax.optimization_barrier((recv, own_weight, sib_weight))
    filtered = convolve(recv, gain)
    returned = lax.all_to_all(filtered, NAMES, split_axis=0, concat_axis=0, tiled=True)
    mixed, upper, lower = apply_gate(returned, gate_signal)

    upper_z = [upper] + [along_z(upper, -step) for step in (1, 2, 3)]
    lower_x = [lower, flip(lower, xh=1)]
    uppers = [[part, flip(part, xh=1)] for part in upper_z]
    lowers = [lower_x] + [[along_z(part, -step) for part in lower_x] for step in (1, 2, 3)]

    core = at["c"].astype(jnp.int32).reshape(1)
    shards = [half[z][xh] for half in (uppers, lowers) for z in range(4) for xh in range(2)]
    messages = project(core, shards, own_weight, sib_weight)
    own = lax.all_to_all(messages, ("xl", "yh", "yl"), split_axis=0, concat_axis=0, tiled=True)
    sib = flip(own, c=1)
    place = jnp.stack([at["yl"], at["z"], at["xh"], at["c"]]).astype(jnp.int32)
    heads = attend(place, own, sib)

    out = lax.all_to_all(heads, ("xl", "yh", "yl", "z", "xh"), split_axis=0, concat_axis=0, tiled=True)
    out = out.reshape(2, 2, 2, 4, 2, 2, PART // 2, HD).transpose(5, 2, 6, 3, 4, 0, 1, 7)
    return mixed, out.reshape(ROWS, CHANS)


def solution(mesh):
    fine = Mesh(mesh.devices.reshape(SIZES), NAMES)
    rows = P(NAMES, None)
    return jax.shard_map(
        per_device,
        mesh=fine,
        in_specs=(rows, rows, rows, rows, P(), P(None, ("z", "xh", "c"), None)),
        out_specs=(rows, rows),
        check_vma=False,
    )
```

```python
import functools
import itertools
import math

import jax
import jax.numpy as jnp
import ml_dtypes
import numpy as np
from jax import lax
from jax.experimental import pallas as pl
from jax.experimental.pallas import tpu as pltpu
from jax.sharding import Mesh, PartitionSpec as P

BF = jnp.bfloat16
F32 = jnp.float32
NAMES = ("xl", "yh", "yl", "z", "xh", "c")
SIZES = (2, 2, 2, 4, 2, 2)
ROWS = 64
DEVS = 128
SEQ = ROWS * DEVS
CHANS = 4096
HALF = CHANS // 2
HD = 128
VMEM_LIMIT = 60 * 1024 * 1024


def split16(table):
    table = np.asarray(table, np.float64)
    high = table.astype(np.float32).astype(ml_dtypes.bfloat16)
    low = (table - high.astype(np.float64)).astype(np.float32).astype(ml_dtypes.bfloat16)
    return high, low


def conv_tables():
    d = np.arange(DEVS)
    k1 = np.arange(DEVS) + 0.25
    r = np.arange(ROWS)
    outer = 2 * math.pi * np.outer(k1, d) / DEVS
    first = np.concatenate([np.cos(outer), -np.sin(outer)], axis=0)
    twist = 2 * math.pi * np.outer(k1, r) / SEQ
    twist_cos = np.tile(np.cos(twist), (1, 2)).astype(np.float32)
    twist_sin = np.tile(np.sin(twist), (1, 2)).astype(np.float32)
    inner = 2 * math.pi * np.outer(r, r) / ROWS
    eye = np.eye(2)
    cos, sin = np.kron(eye, np.cos(inner)), np.kron(eye, np.sin(inner))
    second = np.block([[cos, -sin], [sin, cos]])
    third = np.block([[cos, sin], [-sin, cos]])
    last = np.concatenate([np.cos(outer).T, -np.sin(outer).T], axis=1) / SEQ
    return (*split16(first), twist_cos, twist_sin, *split16(second), *split16(third), *split16(last))


def whole(shape):
    return pl.BlockSpec(shape, lambda *_: (0,) * len(shape), memory_space=pltpu.VMEM)


def params(**more):
    return pltpu.CompilerParams(vmem_limit_bytes=VMEM_LIMIT, **more)


WIDE = CHANS // 16


def pack_kernel(key_ref, value_ref, taps_ref, gate_ref, out_ref, gate_out_ref):
    def both(ref, start):
        return jnp.concatenate(
            [ref[:, pl.ds(start + half * 128, 128)].astype(F32) for half in range(2)], axis=0
        )

    for block in range(16):
        start = block * WIDE
        product = (both(key_ref, start) * both(value_ref, start)).astype(BF).astype(F32)
        for which, tile in enumerate((product, both(taps_ref, start))):
            out_ref[:, block, which] = tile.T.astype(BF).reshape(8, 16, 128)
        gate_out_ref[block] = gate_ref[:, pl.ds(start, WIDE)]


def pack(key_signal, value_signal, long_filter, gate_signal):
    shapes = [(8, 16, 2, 16, 128), (16, ROWS, WIDE)]
    return pl.pallas_call(
        pack_kernel,
        out_shape=[jax.ShapeDtypeStruct(shape, BF) for shape in shapes],
        in_specs=[whole((ROWS, CHANS))] * 4,
        out_specs=[whole(shape) for shape in shapes],
        compiler_params=params(),
        name="pack",
    )(key_signal, value_signal, long_filter, gate_signal)


def dot(a, b):
    return jnp.dot(a, b, preferred_element_type=F32)


def cut(x):
    high = x.astype(BF)
    return high, (x - high.astype(F32)).astype(BF)


def conv_kernel(
    batch, recv_ref, gain_ref, w1h, w1l, tc_ref, ts_ref, m2h, m2l, m3h, m3l, w3h, w3l, out_ref, x_s, h_s, y_s
):
    x_s[...] = recv_ref[:, 0].astype(F32).reshape(DEVS * 16, 128)
    h_s[...] = recv_ref[:, 1].astype(F32).reshape(DEVS * 16, 128)
    tc = tc_ref[...]
    ts = ts_ref[...]

    def three(a, bh, bl):
        ah, al = cut(a)
        return dot(ah, bh) + (dot(al, bh) + dot(ah, bl))

    def step(it, carry):
        rows = [pl.ds(it * batch + u, DEVS, stride=16) for u in range(batch)]
        xs = [x_s[row, :] for row in rows]
        hs = [h_s[row, :] for row in rows]
        signal = jnp.concatenate([v.astype(BF) for v in xs + hs], axis=1)
        first = dot(w1h[...], signal) + dot(w1l[...], signal)
        stacked = []
        for u in range(2 * batch):
            re = first[:DEVS, u * 128 : u * 128 + 128]
            im = first[DEVS:, u * 128 : u * 128 + 128]
            stacked.append(jnp.concatenate([re * tc + im * ts, im * tc - re * ts], axis=1))
        spectrum = three(jnp.concatenate(stacked, axis=0), m2h[...], m2l[...])
        prods = []
        for u in range(batch):
            s = spectrum[u * 128 : u * 128 + 128]
            h = spectrum[(batch + u) * 128 : (batch + u) * 128 + 128]
            sr, si, hr, hi = s[:, :128], s[:, 128:], h[:, :128], h[:, 128:]
            prods.append(jnp.concatenate([sr * hr - si * hi, sr * hi + si * hr], axis=1))
        back = three(jnp.concatenate(prods, axis=0), m3h[...], m3l[...])
        outs = []
        for u in range(batch):
            re = back[u * 128 : u * 128 + 128, :128]
            im = back[u * 128 : u * 128 + 128, 128:]
            outs.append(jnp.concatenate([re * tc - im * ts, im * tc + re * ts], axis=0))
        vh, vl = cut(jnp.concatenate(outs, axis=1))
        conv = dot(w3h[...], vh) + (dot(w3l[...], vh) + dot(w3h[...], vl))
        for u in range(batch):
            gain = gain_ref[pl.ds(it * batch + u, 1), :]
            y_s[rows[u], :] = conv[:, u * 128 : u * 128 + 128] + gain * xs[u]
        return carry

    lax.fori_loop(0, 16 // batch, step, 0)
    out_ref[...] = y_s[...].reshape(DEVS, 16, 128).astype(BF)


def convolve(recv, gain, batch=16):
    tables = conv_tables()
    args = (recv, gain, *[jnp.asarray(t) for t in tables])
    return pl.pallas_call(
        functools.partial(conv_kernel, batch),
        out_shape=jax.ShapeDtypeStruct((DEVS, 16, 128), BF),
        in_specs=[whole(a.shape) for a in args],
        out_specs=whole((DEVS, 16, 128)),
        scratch_shapes=[pltpu.VMEM((DEVS * 16, 128), F32)] * 3,
        compiler_params=params(),
        name="convolve",
    )(*args)


PART = ROWS // 2
GROUP = 8 * ROWS
ASKED = GROUP // 2
MESSAGE = 2 * GROUP + ASKED


SPOTS = [(half, z, xh) for z in range(4) for xh in range(2) for half in range(2)]
EARLY = [(0, 0, 0), (1, 0, 0), (0, 0, 1), (0, 1, 0), (0, 3, 0), (0, 2, 0), (1, 0, 1), (1, 1, 0)]
LATE = [spot for spot in SPOTS if spot not in EARLY]


def place(at_ref, spot):
    half, z, xh = spot
    return ((at_ref[3] + z) & 3) * 4 + (at_ref[4] ^ xh) * 2 + (at_ref[5] ^ half)


def gate_kernel(at_ref, recv_ref, gate_ref, keep_ref, send_ref):
    for spot in range(16):
        tile = recv_ref[:, spot].astype(F32).reshape(128, 128).T
        wide = jnp.concatenate([tile[:ROWS], tile[ROWS:]], axis=1)
        mixed = (gate_ref[spot].astype(F32) * wide).astype(BF)
        first = spot // 2 * ROWS

        @pl.when(at_ref[5] == spot % 2)
        def _():
            keep_ref[first : first + ROWS] = mixed

        @pl.when(at_ref[5] != spot % 2)
        def _():
            send_ref[first : first + ROWS] = mixed


def apply_gate(at, recv, gate):
    return pl.pallas_call(
        gate_kernel,
        out_shape=[jax.ShapeDtypeStruct((GROUP, WIDE), BF)] * 2,
        in_specs=[pl.BlockSpec(memory_space=pltpu.SMEM), whole((8, 16, 16, 128)), whole((16, ROWS, WIDE))],
        out_specs=[whole((GROUP, WIDE))] * 2,
        compiler_params=params(),
        name="apply_gate",
    )(at, recv, gate)


def collect_kernel(at_ref, *refs):
    blocks, out_ref, sems = refs[:16], refs[16], refs[17]
    copies = []
    for n, block in enumerate(blocks):
        mine = pl.ds(pl.multiple_of((at_ref[3] * 2 + at_ref[4]) * ROWS, ROWS), ROWS)
        there = pl.ds(pl.multiple_of(place(at_ref, SPOTS[n]) * WIDE, WIDE), WIDE)
        copies.append(pltpu.make_async_copy(block.at[mine, :], out_ref.at[:, there], sems.at[n]))
    for copy in copies:
        copy.start()
    for copy in copies:
        copy.wait()


def collect(at, blocks):
    return pl.pallas_call(
        collect_kernel,
        out_shape=jax.ShapeDtypeStruct((ROWS, CHANS), BF),
        in_specs=[pl.BlockSpec(memory_space=pltpu.SMEM)] + [pl.BlockSpec(memory_space=pl.ANY)] * 16,
        out_specs=whole((ROWS, CHANS)),
        scratch_shapes=[pltpu.SemaphoreType.DMA((16,))],
        compiler_params=params(),
        name="collect",
    )(at, *blocks)


def project_kernel(final, at_ref, *refs):
    blocks = refs[:8]
    weights = refs[8:10]
    before = refs[10] if final else None
    out_ref, w_s, sems = refs[-3:]
    copies = []
    for n in range(8):
        for side in range(2):
            first = place(at_ref, (LATE if final else EARLY)[n]) * WIDE
            source = weights[side].at[pl.ds(pl.multiple_of(first, WIDE), WIDE), :]
            target = w_s.at[side, pl.ds(n * WIDE, WIDE), :]
            copies.append(pltpu.make_async_copy(source, target, sems.at[n, side]))
    for copy in copies:
        copy.start()
    total = [None, None]
    for chunk in range(2):
        x = jnp.concatenate([block[...] for block in blocks[chunk * 4 : chunk * 4 + 4]], axis=1)
        for copy in copies[chunk * 8 : chunk * 8 + 8]:
            copy.wait()
        for side in range(2):
            part = dot(x, w_s[side, chunk * 4 * WIDE : chunk * 4 * WIDE + 4 * WIDE])
            total[side] = part if chunk == 0 else total[side] + part
    if not final:
        for side in range(2):
            out_ref[side] = total[side]
        return
    for side in range(2):
        done = total[side] + before[side]
        for yh in range(2):
            start = yh * 3 * HD
            queries = done[:, start : start + HD].astype(BF).reshape(8, 2, PART, HD)
            keys = done[:, start + HD : start + 2 * HD].astype(BF)
            values = done[:, start + 2 * HD : start + 3 * HD]
            flipped = [values[n * HD : n * HD + HD].T.astype(BF) for n in range(GROUP // HD)]
            for yl in range(2):
                goal = (at_ref[5] ^ side) * 4 + yh * 2 + yl
                out_ref[goal, :GROUP] = keys
                for n, tile in enumerate(flipped):
                    out_ref[goal, GROUP + n * HD : GROUP + n * HD + HD] = tile
                out_ref[goal, 2 * GROUP :] = queries[:, yl].reshape(ASKED, HD)


def project(at, blocks, own, sib, before=None):
    share = (2, GROUP, 6 * HD)
    final = before is not None
    out = jax.ShapeDtypeStruct((8, MESSAGE, HD), BF) if final else jax.ShapeDtypeStruct(share, F32)
    return pl.pallas_call(
        functools.partial(project_kernel, final),
        out_shape=out,
        in_specs=[pl.BlockSpec(memory_space=pltpu.SMEM)]
        + [whole((GROUP, WIDE))] * 8
        + [pl.BlockSpec(memory_space=pl.ANY)] * 2
        + [whole(share)] * final,
        out_specs=whole(out.shape),
        scratch_shapes=[pltpu.VMEM((2, 8 * WIDE, 6 * HD), BF), pltpu.SemaphoreType.DMA((8, 2))],
        cost_estimate=pl.CostEstimate(
            flops=GROUP * CHANS * 12 * HD, bytes_accessed=CHANS * 12 * HD, transcendentals=0
        ),
        compiler_params=params(),
        name="project_last" if final else "project_first",
    )(at, *blocks, own, sib, *([before] * final))


SCALE = math.log2(math.e) / math.sqrt(HD)
EXTRA = 16
KEYS = 2 * GROUP
QUERIES = ASKED


PAIR = 2 * QUERIES
ROOM = 80.0
REACH = 170.0


def attend_kernel(at_ref, *refs):
    own_hbm, sib_hbm, out_ref, k_s, v_s, q_s, acc_s, sems = refs
    my_yl, my_c = at_ref[2], at_ref[5]

    def fetch(group):
        copies = []

        def add(source, target):
            copies.append(pltpu.make_async_copy(source, target, sems.at[group, len(copies)]))

        for n, source in enumerate((own_hbm, sib_hbm)):
            add(source.at[group, pl.ds(0, GROUP)], k_s.at[group, pl.ds(n * GROUP, GROUP)])
            for tile in range(GROUP // HD):
                add(
                    source.at[group, pl.ds(GROUP + tile * HD, HD)],
                    v_s.at[group, pl.ds(0, HD), pl.ds(n * GROUP + tile * HD, HD)],
                )
            if n == 0:
                add(source.at[group, pl.ds(2 * GROUP, ASKED)], q_s.at[group])
        return copies

    for group in range(8):
        for copy in fetch(group):
            copy.start()
    for group in range(8):
        v_s[group, HD:] = jnp.ones((EXTRA, KEYS), BF)

    row = lax.broadcasted_iota(jnp.int32, (KEYS, 1), 0)
    col = lax.broadcasted_iota(jnp.int32, (1, PAIR), 1)
    key_pos = ((row >> 6) & 7) * 128 + (my_c ^ (row >> 9)) * ROWS + (row & 63)
    query_pos = (col >> 8) * 1024 + ((col >> 5) & 7) * 128 + my_c * ROWS + my_yl * PART + (col & 31)

    def nt(a, b):
        return lax.dot_general(a, b, (((1,), (1,)), ((), ())), preferred_element_type=F32)

    def score(group, queries, which):
        s = nt(k_s[group], queries)
        if which is not None:
            s = jnp.where(key_pos + which * 1024 <= query_pos, s, -1e30)
        return s

    def pair(k, tallest):
        groups = (2 * k, 2 * k + 1)
        for group in groups:
            for copy in fetch(group):
                copy.wait()
        queries = jnp.concatenate([q_s[group] for group in groups], axis=0)
        itself = jnp.concatenate(
            [
                k_s[group, pl.ds(pl.multiple_of(shard * ROWS + my_yl * PART, PART), PART)]
                for group in groups
                for shard in range(8)
            ],
            axis=0,
        )
        ones = jnp.ones((16, HD), BF)
        for group in groups:
            square = nt(ones, jnp.square(k_s[group].astype(F32)).astype(BF))
            tallest = jnp.maximum(tallest, jnp.max(square[:8], axis=1, keepdims=True))
        size = nt(ones, jnp.square(queries.astype(F32)).astype(BF))[:1]
        bound = jnp.sqrt(size * tallest[:1]) * (SCALE * 1.02)
        product = (queries.astype(F32) * itself.astype(F32)).astype(BF)
        own = nt(ones, product)[:1] * SCALE
        safe = jnp.max(bound * 1.01 - own) <= REACH
        acc_s[...] = jnp.zeros(acc_s.shape, F32)

        @pl.when(safe)
        def _():
            offset = bound - ROOM

            def visit(group, which=None):
                weight = jnp.exp2(score(group, queries, which) * SCALE - offset).astype(BF)
                acc_s[...] += dot(v_s[group], weight)

            visit(groups[0], 0)
            visit(groups[1], 1)

            @pl.loop(0, 2 * k)
            def _(group):
                visit(group)

        @pl.when(jnp.logical_not(safe))
        def _():
            def visit(group, best, which=None):
                s = score(group, queries, which)
                new = jnp.maximum(best, jnp.max(s, axis=0, keepdims=True))
                weight = jnp.exp2((s - new) * SCALE).astype(BF)
                acc_s[...] = acc_s[...] * jnp.exp2((best - new) * SCALE) + dot(v_s[group], weight)
                return new

            best = visit(groups[0], jnp.full((1, PAIR), -1e30, F32), 0)
            best = visit(groups[1], best, 1)
            lax.fori_loop(0, 2 * k, visit, best)

        out = (acc_s[:HD] / acc_s[HD : HD + 1]).T.astype(BF)
        for n, group in enumerate(groups):
            for shard in range(8):
                first = n * QUERIES + shard * PART
                out_ref[group * 8 + shard] = out[first : first + PART]
        return tallest

    lax.fori_loop(0, 4, pair, jnp.zeros((8, 1), F32))


def attend(at, own, sib):
    return pl.pallas_call(
        attend_kernel,
        out_shape=jax.ShapeDtypeStruct((64, PART, HD), BF),
        in_specs=[pl.BlockSpec(memory_space=pltpu.SMEM)] + [pl.BlockSpec(memory_space=pl.ANY)] * 2,
        out_specs=whole((64, PART, HD)),
        scratch_shapes=[
            pltpu.VMEM((8, KEYS, HD), BF),
            pltpu.VMEM((8, HD + EXTRA, KEYS), BF),
            pltpu.VMEM((8, QUERIES, HD), BF),
            pltpu.VMEM((HD + EXTRA, PAIR), F32),
            pltpu.SemaphoreType.DMA((8, 11)),
        ],
        compiler_params=params(),
        name="attend",
    )(at, own, sib)


def shift(x, move):
    pairs = []
    for spot in itertools.product(*[range(n) for n in SIZES]):
        target = dict(zip(NAMES, spot))
        move(target)
        goal = [target[n] % size for n, size in zip(NAMES, SIZES)]
        pairs.append((int(np.ravel_multi_index(spot, SIZES)), int(np.ravel_multi_index(goal, SIZES))))
    return lax.ppermute(x, NAMES, pairs)


def along_z(x, step):
    def move(t):
        t["z"] = (t["z"] + step) % 4

    return shift(x, move)


def flip(x, **bits):
    def move(t):
        for name, bit in bits.items():
            t[name] ^= bit

    return shift(x, move)


def per_device(gate_signal, key_signal, value_signal, long_filter, skip_gain, head_weight):
    at = jnp.stack([lax.axis_index(name) for name in NAMES]).astype(jnp.int32)
    device = lax.axis_index(NAMES)

    packed, gate = pack(key_signal, value_signal, long_filter, gate_signal)
    packed = packed.reshape(DEVS, 2, 16, 128)
    recv = lax.all_to_all(packed, NAMES, split_axis=0, concat_axis=0, tiled=True)

    own_weight = head_weight.reshape(CHANS, 6 * HD)
    sib_weight = flip(head_weight, c=1).reshape(CHANS, 6 * HD)

    inner, outer = device % 16, device // 16
    gain = skip_gain.reshape(16, 2, 8, 16)[inner, :, outer]
    gain = jnp.repeat(gain.T, ROWS, axis=1)
    recv, own_weight, sib_weight, gate, at, gain = lax.optimization_barrier(
        (recv, own_weight, sib_weight, gate, at, gain)
    )
    gate = lax.all_to_all(gate, ("z", "xh", "c"), split_axis=0, concat_axis=0, tiled=True)
    filtered, gate = lax.optimization_barrier((convolve(recv, gain), gate))
    returned = lax.all_to_all(filtered, ("xl", "yh", "yl"), split_axis=0, concat_axis=0, tiled=True)
    kept, sent = apply_gate(at, returned.reshape(8, 16, 16, 128), gate)
    given = flip(sent, c=1)

    def round_z(part, way):
        near, far = along_z(part, -way), along_z(part, way)
        return {0: part, way % 4: near, -way % 4: far, 2: along_z(near, -way)}

    kept_z = round_z(kept, 1)
    given_z = [round_z(given, -1), round_z(flip(given, xh=1), 1)]
    blocks = {}
    for half, z, xh in SPOTS:
        if half == 1:
            blocks[half, z, xh] = given_z[xh][z]
        else:
            blocks[half, z, xh] = flip(kept_z[z], xh=1) if xh else kept_z[z]

    share = project(at, [blocks[spot] for spot in EARLY], own_weight, sib_weight)
    messages = project(at, [blocks[spot] for spot in LATE], own_weight, sib_weight, share)
    mixed = collect(at, [blocks[spot] for spot in SPOTS])

    own = lax.all_to_all(messages, ("xl", "yh", "yl"), split_axis=0, concat_axis=0, tiled=True)
    sib = flip(own, c=1)
    heads = attend(at, own, sib)

    out = lax.all_to_all(heads, ("xl", "yh", "yl", "z", "xh"), split_axis=0, concat_axis=0, tiled=True)
    out = out.reshape(2, 2, 2, 4, 2, PART, HD).transpose(2, 5, 3, 4, 0, 1, 6)
    return mixed, out.reshape(ROWS, CHANS)


def solution(mesh):
    fine = Mesh(mesh.devices.reshape(SIZES), NAMES)
    rows = P(NAMES, None)
    return jax.shard_map(
        per_device,
        mesh=fine,
        in_specs=(rows, rows, rows, rows, P(), P(None, ("z", "xh", "c"), None)),
        out_specs=(rows, rows),
        check_vma=False,
    )
```

```python
import functools
import itertools
import math

import jax
import jax.numpy as jnp
import ml_dtypes
import numpy as np
from jax import lax
from jax.experimental import pallas as pl
from jax.experimental.pallas import tpu as pltpu
from jax.sharding import Mesh, PartitionSpec as P

BF = jnp.bfloat16
F32 = jnp.float32
NAMES = ("xl", "yh", "yl", "z", "xh", "c")
SIZES = (2, 2, 2, 4, 2, 2)
ROWS = 64
DEVS = 128
SEQ = ROWS * DEVS
CHANS = 4096
HALF = CHANS // 2
HD = 128
VMEM_LIMIT = 60 * 1024 * 1024


def split16(table):
    table = np.asarray(table, np.float64)
    high = table.astype(np.float32).astype(ml_dtypes.bfloat16)
    low = (table - high.astype(np.float64)).astype(np.float32).astype(ml_dtypes.bfloat16)
    return high, low


def conv_tables():
    d = np.arange(DEVS)
    k1 = np.arange(DEVS) + 0.25
    r = np.arange(ROWS)
    outer = 2 * math.pi * np.outer(k1, d) / DEVS
    first = np.concatenate([np.cos(outer), -np.sin(outer)], axis=0)
    twist = 2 * math.pi * np.outer(k1, r) / SEQ
    twist_cos = np.tile(np.cos(twist), (1, 2)).astype(np.float32)
    twist_sin = np.tile(np.sin(twist), (1, 2)).astype(np.float32)
    inner = 2 * math.pi * np.outer(r, r) / ROWS
    eye = np.eye(2)
    cos, sin = np.kron(eye, np.cos(inner)), np.kron(eye, np.sin(inner))
    second = np.block([[cos, -sin], [sin, cos]])
    third = np.block([[cos, sin], [-sin, cos]])
    last = np.concatenate([np.cos(outer).T, -np.sin(outer).T], axis=1) / SEQ
    first, second, third, last = [split16(table) for table in (first, second, third, last)]
    return (
        np.concatenate(first, axis=1),
        twist_cos,
        twist_sin,
        np.concatenate([second[0], second[0], second[1]], axis=0),
        np.concatenate([third[0], third[0], third[1]], axis=0),
        np.concatenate([last[0], last[1], last[0]], axis=1),
    )


def whole(shape):
    return pl.BlockSpec(shape, lambda *_: (0,) * len(shape), memory_space=pltpu.VMEM)


def params(**more):
    return pltpu.CompilerParams(vmem_limit_bytes=VMEM_LIMIT, **more)


WIDE = CHANS // 16


def pack_kernel(key_ref, value_ref, taps_ref, gate_ref, out_ref, gate_out_ref):
    def both(ref, start):
        return jnp.concatenate(
            [ref[:, pl.ds(start + half * 128, 128)].astype(F32) for half in range(2)], axis=0
        )

    for block in range(16):
        start = block * WIDE
        product = (both(key_ref, start) * both(value_ref, start)).astype(BF).astype(F32)
        for which, tile in enumerate((product, both(taps_ref, start))):
            out_ref[:, block, which] = tile.T.astype(BF).reshape(8, 16, 128)
        gate_out_ref[block] = gate_ref[:, pl.ds(start, WIDE)]


def pack(key_signal, value_signal, long_filter, gate_signal):
    shapes = [(8, 16, 2, 16, 128), (16, ROWS, WIDE)]
    return pl.pallas_call(
        pack_kernel,
        out_shape=[jax.ShapeDtypeStruct(shape, BF) for shape in shapes],
        in_specs=[whole((ROWS, CHANS))] * 4,
        out_specs=[whole(shape) for shape in shapes],
        compiler_params=params(),
        name="pack",
    )(key_signal, value_signal, long_filter, gate_signal)


def dot(a, b):
    return jnp.dot(a, b, preferred_element_type=F32)


def cut(x):
    high = x.astype(BF)
    return high, (x - high.astype(F32)).astype(BF)


def conv_kernel(
    batch, recv_ref, gain_ref, w1, tc_ref, ts_ref, m2, m3, w3, out_ref, x_s, h_s, y_s
):
    x_s[...] = recv_ref[:, 0].astype(F32).reshape(DEVS * 16, 128)
    h_s[...] = recv_ref[:, 1].astype(F32).reshape(DEVS * 16, 128)
    tc = tc_ref[...]
    ts = ts_ref[...]

    def three(a, b):
        ah, al = cut(a)
        return dot(jnp.concatenate([ah, al, ah], axis=1), b)

    def step(it, carry):
        rows = [pl.ds(it * batch + u, DEVS, stride=16) for u in range(batch)]
        xs = [x_s[row, :] for row in rows]
        hs = [h_s[row, :] for row in rows]
        signal = jnp.concatenate([v.astype(BF) for v in xs + hs], axis=1)
        first = dot(w1[...], jnp.concatenate([signal, signal], axis=0))
        stacked = []
        for u in range(2 * batch):
            re = first[:DEVS, u * 128 : u * 128 + 128]
            im = first[DEVS:, u * 128 : u * 128 + 128]
            stacked.append(jnp.concatenate([re * tc + im * ts, im * tc - re * ts], axis=1))
        spectrum = three(jnp.concatenate(stacked, axis=0), m2[...])
        prods = []
        for u in range(batch):
            s = spectrum[u * 128 : u * 128 + 128]
            h = spectrum[(batch + u) * 128 : (batch + u) * 128 + 128]
            sr, si, hr, hi = s[:, :128], s[:, 128:], h[:, :128], h[:, 128:]
            prods.append(jnp.concatenate([sr * hr - si * hi, sr * hi + si * hr], axis=1))
        back = three(jnp.concatenate(prods, axis=0), m3[...])
        outs = []
        for u in range(batch):
            re = back[u * 128 : u * 128 + 128, :128]
            im = back[u * 128 : u * 128 + 128, 128:]
            outs.append(jnp.concatenate([re * tc - im * ts, im * tc + re * ts], axis=0))
        vh, vl = cut(jnp.concatenate(outs, axis=1))
        conv = dot(w3[...], jnp.concatenate([vh, vh, vl], axis=0))
        for u in range(batch):
            gain = gain_ref[pl.ds(it * batch + u, 1), :]
            y_s[rows[u], :] = conv[:, u * 128 : u * 128 + 128] + gain * xs[u]
        return carry

    lax.fori_loop(0, 16 // batch, step, 0)
    out_ref[...] = y_s[...].reshape(DEVS, 16, 128).astype(BF)


def convolve(recv, gain, batch=16):
    tables = conv_tables()
    args = (recv, gain, *[jnp.asarray(t) for t in tables])
    return pl.pallas_call(
        functools.partial(conv_kernel, batch),
        out_shape=jax.ShapeDtypeStruct((DEVS, 16, 128), BF),
        in_specs=[whole(a.shape) for a in args],
        out_specs=whole((DEVS, 16, 128)),
        scratch_shapes=[pltpu.VMEM((DEVS * 16, 128), F32)] * 3,
        compiler_params=params(),
        name="convolve",
    )(*args)


PART = ROWS // 2
GROUP = 8 * ROWS
ASKED = GROUP // 2
MESSAGE = 2 * GROUP + ASKED


SPOTS = [(half, z, xh) for z in range(4) for xh in range(2) for half in range(2)]
EARLY = [(0, 0, 0), (1, 0, 0), (0, 0, 1), (0, 1, 0), (0, 3, 0), (0, 2, 0), (1, 0, 1), (1, 1, 0)]
STAGES = [EARLY, [spot for spot in SPOTS if spot not in EARLY]]


def place(at_ref, spot):
    half, z, xh = spot
    return ((at_ref[3] + z) & 3) * 4 + (at_ref[4] ^ xh) * 2 + (at_ref[5] ^ half)


def gate_kernel(at_ref, recv_ref, gate_ref, keep_ref, send_ref):
    for side, ref in enumerate((keep_ref, send_ref)):
        for pair in range(8):
            spot = pair * 2 + (at_ref[5] ^ side)
            tile = recv_ref[:, spot].astype(F32).reshape(128, 128).T
            wide = jnp.concatenate([tile[:ROWS], tile[ROWS:]], axis=1)
            ref[pair * ROWS : pair * ROWS + ROWS] = (gate_ref[spot].astype(F32) * wide).astype(BF)


def apply_gate(at, recv, gate):
    return pl.pallas_call(
        gate_kernel,
        out_shape=[jax.ShapeDtypeStruct((GROUP, WIDE), BF)] * 2,
        in_specs=[pl.BlockSpec(memory_space=pltpu.SMEM), whole((8, 16, 16, 128)), whole((16, ROWS, WIDE))],
        out_specs=[whole((GROUP, WIDE))] * 2,
        compiler_params=params(),
        name="apply_gate",
    )(at, recv, gate)


def collect_kernel(at_ref, *refs):
    blocks, out_ref, sems = refs[:16], refs[16], refs[17]
    copies = []
    for n, block in enumerate(blocks):
        mine = pl.ds(pl.multiple_of((at_ref[3] * 2 + at_ref[4]) * ROWS, ROWS), ROWS)
        there = pl.ds(pl.multiple_of(place(at_ref, SPOTS[n]) * WIDE, WIDE), WIDE)
        copies.append(pltpu.make_async_copy(block.at[mine, :], out_ref.at[:, there], sems.at[n]))
    for copy in copies:
        copy.start()
    for copy in copies:
        copy.wait()


def collect(at, blocks):
    return pl.pallas_call(
        collect_kernel,
        out_shape=jax.ShapeDtypeStruct((ROWS, CHANS), BF),
        in_specs=[pl.BlockSpec(memory_space=pltpu.SMEM)] + [pl.BlockSpec(memory_space=pl.ANY)] * 16,
        out_specs=whole((ROWS, CHANS)),
        scratch_shapes=[pltpu.SemaphoreType.DMA((16,))],
        compiler_params=params(),
        name="collect",
    )(at, *blocks)


def project_kernel(stage, at_ref, *refs):
    spots = STAGES[stage]
    first, last = stage == 0, stage == len(STAGES) - 1
    blocks, refs = refs[: len(spots)], refs[len(spots) :]
    weights, refs = refs[:2], refs[2:]
    before, refs = (None, refs) if first else (refs[0], refs[1:])
    out_ref, x_s, w_s, acc, goal_s, load_sems, save_sems = refs
    loads = []

    def load(source, target):
        loads.append(pltpu.make_async_copy(source, target, load_sems.at[len(loads)]))
        loads[-1].start()

    for n, block in enumerate(blocks):
        load(block, x_s.at[:, pl.ds(n * WIDE, WIDE)])
    for side in range(2):
        for n, spot in enumerate(spots):
            rows = pl.ds(pl.multiple_of(place(at_ref, spot) * WIDE, WIDE), WIDE)
            load(weights[side].at[rows, :], w_s.at[side, pl.ds(n * WIDE, WIDE)])
        if not first:
            load(before.at[side], acc.at[side])
    per_side = len(spots) + (not first)
    for copy in loads[: len(spots)]:
        copy.wait()

    saves = []

    def save(source, target):
        saves.append(pltpu.make_async_copy(source, target, save_sems.at[len(saves)]))
        saves[-1].start()

    for side in range(2):
        for copy in loads[len(spots) + side * per_side : len(spots) + (side + 1) * per_side]:
            copy.wait()
        done = dot(x_s[...], w_s[side])
        if not first:
            done = done + acc[side]
        if not last:
            acc[side] = done
            save(acc.at[side], out_ref.at[side])
            continue
        for yh in range(2):
            start = yh * 3 * HD
            queries = done[:, start : start + HD].astype(BF).reshape(8, 2, PART, HD)
            keys = done[:, start + HD : start + 2 * HD].astype(BF)
            values = done[:, start + 2 * HD : start + 3 * HD]
            flipped = [values[n * HD : n * HD + HD].T.astype(BF) for n in range(GROUP // HD)]
            for yl in range(2):
                slot = side * 4 + yh * 2 + yl
                goal_s[slot, :GROUP] = keys
                for n, tile in enumerate(flipped):
                    goal_s[slot, GROUP + n * HD : GROUP + n * HD + HD] = tile
                goal_s[slot, 2 * GROUP :] = queries[:, yl].reshape(ASKED, HD)
                save(goal_s.at[slot], out_ref.at[(at_ref[5] ^ side) * 4 + yh * 2 + yl])
    for copy in saves:
        copy.wait()


def project(stage, at, blocks, own, sib, before=None):
    share = (2, GROUP, 6 * HD)
    message = (8, MESSAGE, HD)
    last = stage == len(STAGES) - 1
    count = len(blocks)
    return pl.pallas_call(
        functools.partial(project_kernel, stage),
        out_shape=jax.ShapeDtypeStruct(message, BF) if last else jax.ShapeDtypeStruct(share, F32),
        in_specs=[pl.BlockSpec(memory_space=pltpu.SMEM)]
        + [pl.BlockSpec(memory_space=pl.ANY)] * (count + 2 + (stage > 0)),
        out_specs=pl.BlockSpec(memory_space=pl.ANY),
        scratch_shapes=[
            pltpu.VMEM((GROUP, count * WIDE), BF),
            pltpu.VMEM((2, count * WIDE, 6 * HD), BF),
            pltpu.VMEM(share, F32),
            pltpu.VMEM(message if last else (8, 16, HD), BF),
            pltpu.SemaphoreType.DMA((3 * count + 2,)),
            pltpu.SemaphoreType.DMA((8,)),
        ],
        cost_estimate=pl.CostEstimate(
            flops=2 * GROUP * count * WIDE * 12 * HD, bytes_accessed=count * WIDE * 24 * HD, transcendentals=0
        ),
        compiler_params=params(),
        name="project_%d" % stage,
    )(at, *blocks, own, sib, *([before] if stage else []))


SCALE = math.log2(math.e) / math.sqrt(HD)
EXTRA = 16
SPAN = 2 * GROUP
KEYS = 2 * SPAN
PAIR = 2 * ASKED
ROOM = 80.0
REACH = 170.0


def attend_kernel(at_ref, *refs):
    own_hbm, sib_hbm, out_ref, k_s, v_s, q_s, acc_s, sems = refs
    my_yl, my_c = at_ref[2], at_ref[5]

    def fetch(k):
        copies = []

        def add(source, target):
            copies.append(pltpu.make_async_copy(source, target, sems.at[k, len(copies)]))

        for n in range(2):
            for side, source in enumerate((own_hbm, sib_hbm)):
                here = source.at[2 * k + n]
                first = n * SPAN + side * GROUP
                add(here.at[pl.ds(0, GROUP)], k_s.at[k, pl.ds(first, GROUP)])
                for tile in range(GROUP // HD):
                    add(
                        here.at[pl.ds(GROUP + tile * HD, HD)],
                        v_s.at[k, pl.ds(0, HD), pl.ds(first + tile * HD, HD)],
                    )
                if side == 0:
                    add(here.at[pl.ds(2 * GROUP, ASKED)], q_s.at[k, pl.ds(n * ASKED, ASKED)])
        return copies

    for k in range(4):
        for copy in fetch(k):
            copy.start()
    for k in range(4):
        v_s[k, HD:] = jnp.ones((EXTRA, KEYS), BF)

    row = lax.broadcasted_iota(jnp.int32, (KEYS, 1), 0)
    col = lax.broadcasted_iota(jnp.int32, (1, PAIR), 1)
    key_pos = (
        (row >> 10) * 1024 + ((row >> 6) & 7) * 128 + (my_c ^ ((row >> 9) & 1)) * ROWS + (row & 63)
    )
    query_pos = (col >> 8) * 1024 + ((col >> 5) & 7) * 128 + my_c * ROWS + my_yl * PART + (col & 31)

    def nt(a, b):
        return lax.dot_general(a, b, (((1,), (1,)), ((), ())), preferred_element_type=F32)

    def pair(k, tallest):
        for copy in fetch(k):
            copy.wait()
        queries = q_s[k]
        itself = jnp.concatenate(
            [
                k_s[k, pl.ds(pl.multiple_of(n * SPAN + shard * ROWS + my_yl * PART, PART), PART)]
                for n in range(2)
                for shard in range(8)
            ],
            axis=0,
        )
        ones = jnp.ones((16, HD), BF)
        square = nt(ones, jnp.square(k_s[k].astype(F32)).astype(BF))
        tallest = jnp.maximum(tallest, jnp.max(square[:8], axis=1, keepdims=True))
        size = nt(ones, jnp.square(queries.astype(F32)).astype(BF))[:1]
        bound = jnp.sqrt(size * tallest[:1]) * (SCALE * 1.02)
        product = (queries.astype(F32) * itself.astype(F32)).astype(BF)
        own = nt(ones, product)[:1] * SCALE
        safe = jnp.max(bound * 1.01 - own) <= REACH

        def score(j, masked):
            s = nt(k_s[j], queries)
            return jnp.where(key_pos <= query_pos, s, -1e30) if masked else s

        @pl.when(safe)
        def _():
            offset = bound - ROOM

            def visit(j, masked=False):
                weight = jnp.exp2(score(j, masked) * SCALE - offset).astype(BF)
                return dot(v_s[j], weight)

            acc_s[...] = visit(k, True)

            @pl.loop(0, k)
            def _(j):
                acc_s[...] += visit(j)

        @pl.when(jnp.logical_not(safe))
        def _():
            def visit(j, best, masked=False):
                s = score(j, masked)
                new = jnp.maximum(best, jnp.max(s, axis=0, keepdims=True))
                weight = jnp.exp2((s - new) * SCALE).astype(BF)
                acc_s[...] = acc_s[...] * jnp.exp2((best - new) * SCALE) + dot(v_s[j], weight)
                return new

            acc_s[...] = jnp.zeros(acc_s.shape, F32)
            best = visit(k, jnp.full((1, PAIR), -1e30, F32), True)
            lax.fori_loop(0, k, visit, best)

        out = (acc_s[:HD] / acc_s[HD : HD + 1]).T.astype(BF)
        for n in range(2):
            for shard in range(8):
                first = n * ASKED + shard * PART
                out_ref[(2 * k + n) * 8 + shard] = out[first : first + PART]
        return tallest

    lax.fori_loop(0, 4, pair, jnp.zeros((8, 1), F32))


def attend(at, own, sib):
    return pl.pallas_call(
        attend_kernel,
        out_shape=jax.ShapeDtypeStruct((64, PART, HD), BF),
        in_specs=[pl.BlockSpec(memory_space=pltpu.SMEM)] + [pl.BlockSpec(memory_space=pl.ANY)] * 2,
        out_specs=whole((64, PART, HD)),
        scratch_shapes=[
            pltpu.VMEM((4, KEYS, HD), BF),
            pltpu.VMEM((4, HD + EXTRA, KEYS), BF),
            pltpu.VMEM((4, PAIR, HD), BF),
            pltpu.VMEM((HD + EXTRA, PAIR), F32),
            pltpu.SemaphoreType.DMA((4, 22)),
        ],
        compiler_params=params(),
        name="attend",
    )(at, own, sib)


def shift(x, move):
    pairs = []
    for spot in itertools.product(*[range(n) for n in SIZES]):
        target = dict(zip(NAMES, spot))
        move(target)
        goal = [target[n] % size for n, size in zip(NAMES, SIZES)]
        pairs.append((int(np.ravel_multi_index(spot, SIZES)), int(np.ravel_multi_index(goal, SIZES))))
    return lax.ppermute(x, NAMES, pairs)


def along_z(x, step):
    def move(t):
        t["z"] = (t["z"] + step) % 4

    return shift(x, move)


def flip(x, **bits):
    def move(t):
        for name, bit in bits.items():
            t[name] ^= bit

    return shift(x, move)


def per_device(gate_signal, key_signal, value_signal, long_filter, skip_gain, head_weight):
    at = jnp.stack([lax.axis_index(name) for name in NAMES]).astype(jnp.int32)
    device = lax.axis_index(NAMES)

    packed, gate = pack(key_signal, value_signal, long_filter, gate_signal)
    packed = packed.reshape(DEVS, 2, 16, 128)
    recv = lax.all_to_all(packed, NAMES, split_axis=0, concat_axis=0, tiled=True)

    own_weight = head_weight.reshape(CHANS, 6 * HD)
    sib_weight = flip(head_weight, c=1).reshape(CHANS, 6 * HD)

    inner, outer = device % 16, device // 16
    gain = skip_gain.reshape(16, 2, 8, 16)[inner, :, outer]
    gain = jnp.repeat(gain.T, ROWS, axis=1)
    recv, own_weight, sib_weight, gate, at, gain = lax.optimization_barrier(
        (recv, own_weight, sib_weight, gate, at, gain)
    )
    gate = lax.all_to_all(gate, ("z", "xh", "c"), split_axis=0, concat_axis=0, tiled=True)
    filtered, gate = lax.optimization_barrier((convolve(recv, gain), gate))
    returned = lax.all_to_all(filtered, ("xl", "yh", "yl"), split_axis=0, concat_axis=0, tiled=True)
    kept, sent = apply_gate(at, returned.reshape(8, 16, 16, 128), gate)
    given = flip(sent, c=1)

    def round_z(part, way):
        near, far = along_z(part, -way), along_z(part, way)
        return {0: part, way % 4: near, -way % 4: far, 2: along_z(near, -way)}

    kept_z = round_z(kept, 1)
    given_z = [round_z(given, -1), round_z(flip(given, xh=1), 1)]
    blocks = {}
    for half, z, xh in SPOTS:
        if half == 1:
            blocks[half, z, xh] = given_z[xh][z]
        else:
            blocks[half, z, xh] = flip(kept_z[z], xh=1) if xh else kept_z[z]

    share = None
    for stage, spots in enumerate(STAGES):
        share = project(stage, at, [blocks[spot] for spot in spots], own_weight, sib_weight, share)
    mixed = collect(at, [blocks[spot] for spot in SPOTS])

    own = lax.all_to_all(share, ("xl", "yh", "yl"), split_axis=0, concat_axis=0, tiled=True)
    sib = flip(own, c=1)
    heads = attend(at, own, sib)

    out = lax.all_to_all(heads, ("xl", "yh", "yl", "z", "xh"), split_axis=0, concat_axis=0, tiled=True)
    out = out.reshape(2, 2, 2, 4, 2, PART, HD).transpose(2, 5, 3, 4, 0, 1, 6)
    return mixed, out.reshape(ROWS, CHANS)


def solution(mesh):
    fine = Mesh(mesh.devices.reshape(SIZES), NAMES)
    rows = P(NAMES, None)
    return jax.shard_map(
        per_device,
        mesh=fine,
        in_specs=(rows, rows, rows, rows, P(), P(None, ("z", "xh", "c"), None)),
        out_specs=(rows, rows),
        check_vma=False,
    )
```

```python
import functools
import itertools
import math

import jax
import jax.numpy as jnp
import ml_dtypes
import numpy as np
from jax import lax
from jax.experimental import pallas as pl
from jax.experimental.pallas import tpu as pltpu
from jax.sharding import Mesh, PartitionSpec as P

BF = jnp.bfloat16
F32 = jnp.float32
NAMES = ("xl", "yh", "yl", "z", "xh", "c")
SIZES = (2, 2, 2, 4, 2, 2)
ROWS = 64
DEVS = 128
SEQ = ROWS * DEVS
CHANS = 4096
HALF = CHANS // 2
HD = 128
VMEM_LIMIT = 60 * 1024 * 1024


def split16(table):
    table = np.asarray(table, np.float64)
    high = table.astype(np.float32).astype(ml_dtypes.bfloat16)
    low = (table - high.astype(np.float64)).astype(np.float32).astype(ml_dtypes.bfloat16)
    return high, low


def conv_tables():
    d = np.arange(DEVS)
    k1 = np.arange(DEVS) + 0.25
    r = np.arange(ROWS)
    outer = 2 * math.pi * np.outer(k1, d) / DEVS
    first = np.concatenate([np.cos(outer), -np.sin(outer)], axis=0)
    twist = 2 * math.pi * np.outer(k1, r) / SEQ
    twist_cos = np.tile(np.cos(twist), (1, 2)).astype(np.float32)
    twist_sin = np.tile(np.sin(twist), (1, 2)).astype(np.float32)
    inner = 2 * math.pi * np.outer(r, r) / ROWS
    eye = np.eye(2)
    cos, sin = np.kron(eye, np.cos(inner)), np.kron(eye, np.sin(inner))
    second = np.block([[cos, -sin], [sin, cos]])
    third = np.block([[cos, sin], [-sin, cos]])
    last = np.concatenate([np.cos(outer).T, -np.sin(outer).T], axis=1) / SEQ
    first, second, third, last = [split16(table) for table in (first, second, third, last)]
    return (
        np.concatenate(first, axis=1),
        twist_cos,
        twist_sin,
        np.concatenate([second[0], second[0], second[1]], axis=0),
        np.concatenate([third[0], third[0], third[1]], axis=0),
        np.concatenate([last[0], last[1], last[0]], axis=1),
    )


def whole(shape):
    return pl.BlockSpec(shape, lambda *_: (0,) * len(shape), memory_space=pltpu.VMEM)


def params(**more):
    return pltpu.CompilerParams(vmem_limit_bytes=VMEM_LIMIT, **more)


WIDE = CHANS // 16


def pack_kernel(key_ref, value_ref, taps_ref, gate_ref, out_ref, gate_out_ref):
    def both(ref, start):
        return jnp.concatenate(
            [ref[:, pl.ds(start + half * 128, 128)].astype(F32) for half in range(2)], axis=0
        )

    for block in range(16):
        start = block * WIDE
        product = (both(key_ref, start) * both(value_ref, start)).astype(BF).astype(F32)
        for which, tile in enumerate((product, both(taps_ref, start))):
            out_ref[:, block, which] = tile.T.astype(BF).reshape(8, 16, 128)
        gate_out_ref[block] = gate_ref[:, pl.ds(start, WIDE)]


def pack(key_signal, value_signal, long_filter, gate_signal):
    shapes = [(8, 16, 2, 16, 128), (16, ROWS, WIDE)]
    return pl.pallas_call(
        pack_kernel,
        out_shape=[jax.ShapeDtypeStruct(shape, BF) for shape in shapes],
        in_specs=[whole((ROWS, CHANS))] * 4,
        out_specs=[whole(shape) for shape in shapes],
        compiler_params=params(),
        name="pack",
    )(key_signal, value_signal, long_filter, gate_signal)


def dot(a, b):
    return jnp.dot(a, b, preferred_element_type=F32)


def cut(x):
    high = x.astype(BF)
    return high, (x - high.astype(F32)).astype(BF)


def conv_kernel(
    batch, recv_ref, gain_ref, w1, tc_ref, ts_ref, m2, m3, w3, out_ref, x_s, h_s, y_s
):
    x_s[...] = recv_ref[:, 0].astype(F32).reshape(DEVS * 16, 128)
    h_s[...] = recv_ref[:, 1].astype(F32).reshape(DEVS * 16, 128)
    tc = tc_ref[...]
    ts = ts_ref[...]

    def three(a, b):
        ah, al = cut(a)
        return dot(jnp.concatenate([ah, al, ah], axis=1), b)

    def step(it, carry):
        rows = [pl.ds(it * batch + u, DEVS, stride=16) for u in range(batch)]
        xs = [x_s[row, :] for row in rows]
        hs = [h_s[row, :] for row in rows]
        signal = jnp.concatenate([v.astype(BF) for v in xs + hs], axis=1)
        first = dot(w1[...], jnp.concatenate([signal, signal], axis=0))
        stacked = []
        for u in range(2 * batch):
            re = first[:DEVS, u * 128 : u * 128 + 128]
            im = first[DEVS:, u * 128 : u * 128 + 128]
            stacked.append(jnp.concatenate([re * tc + im * ts, im * tc - re * ts], axis=1))
        spectrum = three(jnp.concatenate(stacked, axis=0), m2[...])
        prods = []
        for u in range(batch):
            s = spectrum[u * 128 : u * 128 + 128]
            h = spectrum[(batch + u) * 128 : (batch + u) * 128 + 128]
            sr, si, hr, hi = s[:, :128], s[:, 128:], h[:, :128], h[:, 128:]
            prods.append(jnp.concatenate([sr * hr - si * hi, sr * hi + si * hr], axis=1))
        back = three(jnp.concatenate(prods, axis=0), m3[...])
        outs = []
        for u in range(batch):
            re = back[u * 128 : u * 128 + 128, :128]
            im = back[u * 128 : u * 128 + 128, 128:]
            outs.append(jnp.concatenate([re * tc - im * ts, im * tc + re * ts], axis=0))
        vh, vl = cut(jnp.concatenate(outs, axis=1))
        conv = dot(w3[...], jnp.concatenate([vh, vh, vl], axis=0))
        for u in range(batch):
            gain = gain_ref[pl.ds(it * batch + u, 1), :]
            y_s[rows[u], :] = conv[:, u * 128 : u * 128 + 128] + gain * xs[u]
        return carry

    lax.fori_loop(0, 16 // batch, step, 0)
    out_ref[...] = y_s[...].reshape(DEVS, 16, 128).astype(BF)


def convolve(recv, gain, batch=16):
    tables = conv_tables()
    args = (recv, gain, *[jnp.asarray(t) for t in tables])
    return pl.pallas_call(
        functools.partial(conv_kernel, batch),
        out_shape=jax.ShapeDtypeStruct((DEVS, 16, 128), BF),
        in_specs=[whole(a.shape) for a in args],
        out_specs=whole((DEVS, 16, 128)),
        scratch_shapes=[pltpu.VMEM((DEVS * 16, 128), F32)] * 3,
        compiler_params=params(),
        name="convolve",
    )(*args)


PART = ROWS // 2
GROUP = 8 * ROWS
ASKED = GROUP // 2
MESSAGE = 2 * GROUP + ASKED


SPOTS = [(half, z, xh) for z in range(4) for xh in range(2) for half in range(2)]
EARLY = [(0, 0, 0), (1, 0, 0), (0, 0, 1), (0, 1, 0), (0, 3, 0), (0, 2, 0), (1, 0, 1), (1, 1, 0), (1, 3, 0), (0, 1, 1)]
STAGES = [EARLY, [spot for spot in SPOTS if spot not in EARLY]]


def place(at_ref, spot):
    half, z, xh = spot
    return ((at_ref[3] + z) & 3) * 4 + (at_ref[4] ^ xh) * 2 + (at_ref[5] ^ half)


def gate_kernel(at_ref, recv_ref, gate_ref, keep_ref, send_ref):
    for side, ref in enumerate((keep_ref, send_ref)):
        for pair in range(8):
            spot = pair * 2 + (at_ref[5] ^ side)
            tile = recv_ref[:, spot].astype(F32).reshape(128, 128).T
            wide = jnp.concatenate([tile[:ROWS], tile[ROWS:]], axis=1)
            ref[pair * ROWS : pair * ROWS + ROWS] = (gate_ref[spot].astype(F32) * wide).astype(BF)


def apply_gate(at, recv, gate):
    return pl.pallas_call(
        gate_kernel,
        out_shape=[jax.ShapeDtypeStruct((GROUP, WIDE), BF)] * 2,
        in_specs=[pl.BlockSpec(memory_space=pltpu.SMEM), whole((8, 16, 16, 128)), whole((16, ROWS, WIDE))],
        out_specs=[whole((GROUP, WIDE))] * 2,
        compiler_params=params(),
        name="apply_gate",
    )(at, recv, gate)


def collect_kernel(at_ref, *refs):
    blocks, out_ref, sems = refs[:16], refs[16], refs[17]
    copies = []
    for n, block in enumerate(blocks):
        mine = pl.ds(pl.multiple_of((at_ref[3] * 2 + at_ref[4]) * ROWS, ROWS), ROWS)
        there = pl.ds(pl.multiple_of(place(at_ref, SPOTS[n]) * WIDE, WIDE), WIDE)
        copies.append(pltpu.make_async_copy(block.at[mine, :], out_ref.at[:, there], sems.at[n]))
    for copy in copies:
        copy.start()
    for copy in copies:
        copy.wait()


def collect(at, blocks):
    return pl.pallas_call(
        collect_kernel,
        out_shape=jax.ShapeDtypeStruct((ROWS, CHANS), BF),
        in_specs=[pl.BlockSpec(memory_space=pltpu.SMEM)] + [pl.BlockSpec(memory_space=pl.ANY)] * 16,
        out_specs=whole((ROWS, CHANS)),
        scratch_shapes=[pltpu.SemaphoreType.DMA((16,))],
        compiler_params=params(),
        name="collect",
    )(at, *blocks)


def project_kernel(stage, at_ref, *refs):
    spots = STAGES[stage]
    first, last = stage == 0, stage == len(STAGES) - 1
    blocks, refs = refs[: len(spots)], refs[len(spots) :]
    weights, refs = refs[:2], refs[2:]
    before, refs = (None, refs) if first else (refs[0], refs[1:])
    out_ref, x_s, w_s, acc, goal_s, load_sems, save_sems = refs
    loads = []

    def load(source, target):
        loads.append(pltpu.make_async_copy(source, target, load_sems.at[len(loads)]))
        loads[-1].start()

    for n, block in enumerate(blocks):
        load(block, x_s.at[:, pl.ds(n * WIDE, WIDE)])
    for side in range(2):
        for n, spot in enumerate(spots):
            rows = pl.ds(pl.multiple_of(place(at_ref, spot) * WIDE, WIDE), WIDE)
            load(weights[side].at[rows, :], w_s.at[side, pl.ds(n * WIDE, WIDE)])
        if not first:
            load(before.at[side], acc.at[side])
    per_side = len(spots) + (not first)
    for copy in loads[: len(spots)]:
        copy.wait()

    saves = []

    def save(source, target):
        saves.append(pltpu.make_async_copy(source, target, save_sems.at[len(saves)]))
        saves[-1].start()

    for side in range(2):
        for copy in loads[len(spots) + side * per_side : len(spots) + (side + 1) * per_side]:
            copy.wait()
        done = dot(x_s[...], w_s[side])
        if not first:
            done = done + acc[side]
        if not last:
            acc[side] = done
            save(acc.at[side], out_ref.at[side])
            continue
        for yh in range(2):
            start = yh * 3 * HD
            queries = done[:, start : start + HD].astype(BF).reshape(8, 2, PART, HD)
            keys = done[:, start + HD : start + 2 * HD].astype(BF)
            values = done[:, start + 2 * HD : start + 3 * HD]
            flipped = [values[n * HD : n * HD + HD].T.astype(BF) for n in range(GROUP // HD)]
            for yl in range(2):
                slot = side * 4 + yh * 2 + yl
                goal_s[slot, :GROUP] = keys
                for n, tile in enumerate(flipped):
                    goal_s[slot, GROUP + n * HD : GROUP + n * HD + HD] = tile
                goal_s[slot, 2 * GROUP :] = queries[:, yl].reshape(ASKED, HD)
                save(goal_s.at[slot], out_ref.at[(at_ref[5] ^ side) * 4 + yh * 2 + yl])
    for copy in saves:
        copy.wait()


def project(stage, at, blocks, own, sib, before=None):
    share = (2, GROUP, 6 * HD)
    message = (8, MESSAGE, HD)
    last = stage == len(STAGES) - 1
    count = len(blocks)
    return pl.pallas_call(
        functools.partial(project_kernel, stage),
        out_shape=jax.ShapeDtypeStruct(message, BF) if last else jax.ShapeDtypeStruct(share, F32),
        in_specs=[pl.BlockSpec(memory_space=pltpu.SMEM)]
        + [pl.BlockSpec(memory_space=pl.ANY)] * (count + 2 + (stage > 0)),
        out_specs=pl.BlockSpec(memory_space=pl.ANY),
        scratch_shapes=[
            pltpu.VMEM((GROUP, count * WIDE), BF),
            pltpu.VMEM((2, count * WIDE, 6 * HD), BF),
            pltpu.VMEM(share, F32),
            pltpu.VMEM(message if last else (8, 16, HD), BF),
            pltpu.SemaphoreType.DMA((3 * count + 2,)),
            pltpu.SemaphoreType.DMA((8,)),
        ],
        cost_estimate=pl.CostEstimate(
            flops=2 * GROUP * count * WIDE * 12 * HD, bytes_accessed=count * WIDE * 24 * HD, transcendentals=0
        ),
        compiler_params=params(),
        name="project_%d" % stage,
    )(at, *blocks, own, sib, *([before] if stage else []))


SCALE = math.log2(math.e) / math.sqrt(HD)
EXTRA = 16
SPAN = 2 * GROUP
KEYS = 2 * SPAN
PAIR = 2 * ASKED
ROOM = 80.0
REACH = 170.0


def attend_kernel(at_ref, *refs):
    own_hbm, sib_hbm, out_ref, k_s, v_s, q_s, acc_s, sems = refs
    my_yl, my_c = at_ref[2], at_ref[5]

    def fetch(k):
        copies = []

        def add(source, target):
            copies.append(pltpu.make_async_copy(source, target, sems.at[k, len(copies)]))

        for n in range(2):
            for side, source in enumerate((own_hbm, sib_hbm)):
                here = source.at[2 * k + n]
                first = n * SPAN + side * GROUP
                add(here.at[pl.ds(0, GROUP)], k_s.at[k, pl.ds(first, GROUP)])
                for tile in range(GROUP // HD):
                    add(
                        here.at[pl.ds(GROUP + tile * HD, HD)],
                        v_s.at[k, pl.ds(0, HD), pl.ds(first + tile * HD, HD)],
                    )
                if side == 0:
                    add(here.at[pl.ds(2 * GROUP, ASKED)], q_s.at[k, pl.ds(n * ASKED, ASKED)])
        return copies

    for k in range(4):
        for copy in fetch(k):
            copy.start()
    for k in range(4):
        v_s[k, HD:] = jnp.ones((EXTRA, KEYS), BF)

    row = lax.broadcasted_iota(jnp.int32, (KEYS, 1), 0)
    col = lax.broadcasted_iota(jnp.int32, (1, PAIR), 1)
    key_pos = (
        (row >> 10) * 1024 + ((row >> 6) & 7) * 128 + (my_c ^ ((row >> 9) & 1)) * ROWS + (row & 63)
    )
    query_pos = (col >> 8) * 1024 + ((col >> 5) & 7) * 128 + my_c * ROWS + my_yl * PART + (col & 31)

    def nt(a, b):
        return lax.dot_general(a, b, (((1,), (1,)), ((), ())), preferred_element_type=F32)

    def pair(k, tallest):
        for copy in fetch(k):
            copy.wait()
        queries = q_s[k]
        itself = jnp.concatenate(
            [
                k_s[k, pl.ds(pl.multiple_of(n * SPAN + shard * ROWS + my_yl * PART, PART), PART)]
                for n in range(2)
                for shard in range(8)
            ],
            axis=0,
        )
        ones = jnp.ones((16, HD), BF)
        square = nt(ones, jnp.square(k_s[k].astype(F32)).astype(BF))
        tallest = jnp.maximum(tallest, jnp.max(square[:8], axis=1, keepdims=True))
        size = nt(ones, jnp.square(queries.astype(F32)).astype(BF))[:1]
        bound = jnp.sqrt(size * tallest[:1]) * (SCALE * 1.02)
        product = (queries.astype(F32) * itself.astype(F32)).astype(BF)
        own = nt(ones, product)[:1] * SCALE
        safe = jnp.max(bound * 1.01 - own) <= REACH

        def score(j, masked):
            s = nt(k_s[j], queries)
            return jnp.where(key_pos <= query_pos, s, -1e30) if masked else s

        @pl.when(safe)
        def _():
            offset = bound - ROOM

            def visit(j, masked=False):
                weight = jnp.exp2(score(j, masked) * SCALE - offset).astype(BF)
                return dot(v_s[j], weight)

            acc_s[...] = visit(k, True)

            @pl.loop(0, k)
            def _(j):
                acc_s[...] += visit(j)

        @pl.when(jnp.logical_not(safe))
        def _():
            def visit(j, best, masked=False):
                s = score(j, masked)
                new = jnp.maximum(best, jnp.max(s, axis=0, keepdims=True))
                weight = jnp.exp2((s - new) * SCALE).astype(BF)
                acc_s[...] = acc_s[...] * jnp.exp2((best - new) * SCALE) + dot(v_s[j], weight)
                return new

            acc_s[...] = jnp.zeros(acc_s.shape, F32)
            best = visit(k, jnp.full((1, PAIR), -1e30, F32), True)
            lax.fori_loop(0, k, visit, best)

        out = (acc_s[:HD] / acc_s[HD : HD + 1]).T.astype(BF)
        for n in range(2):
            for shard in range(8):
                first = n * ASKED + shard * PART
                out_ref[(2 * k + n) * 8 + shard] = out[first : first + PART]
        return tallest

    lax.fori_loop(0, 4, pair, jnp.zeros((8, 1), F32))


def attend(at, own, sib):
    return pl.pallas_call(
        attend_kernel,
        out_shape=jax.ShapeDtypeStruct((64, PART, HD), BF),
        in_specs=[pl.BlockSpec(memory_space=pltpu.SMEM)] + [pl.BlockSpec(memory_space=pl.ANY)] * 2,
        out_specs=whole((64, PART, HD)),
        scratch_shapes=[
            pltpu.VMEM((4, KEYS, HD), BF),
            pltpu.VMEM((4, HD + EXTRA, KEYS), BF),
            pltpu.VMEM((4, PAIR, HD), BF),
            pltpu.VMEM((HD + EXTRA, PAIR), F32),
            pltpu.SemaphoreType.DMA((4, 22)),
        ],
        compiler_params=params(),
        name="attend",
    )(at, own, sib)


def shift(x, move):
    pairs = []
    for spot in itertools.product(*[range(n) for n in SIZES]):
        target = dict(zip(NAMES, spot))
        move(target)
        goal = [target[n] % size for n, size in zip(NAMES, SIZES)]
        pairs.append((int(np.ravel_multi_index(spot, SIZES)), int(np.ravel_multi_index(goal, SIZES))))
    return lax.ppermute(x, NAMES, pairs)


def along_z(x, step):
    def move(t):
        t["z"] = (t["z"] + step) % 4

    return shift(x, move)


def flip(x, **bits):
    def move(t):
        for name, bit in bits.items():
            t[name] ^= bit

    return shift(x, move)


def per_device(gate_signal, key_signal, value_signal, long_filter, skip_gain, head_weight):
    at = jnp.stack([lax.axis_index(name) for name in NAMES]).astype(jnp.int32)
    device = lax.axis_index(NAMES)

    packed, gate = pack(key_signal, value_signal, long_filter, gate_signal)
    packed = packed.reshape(DEVS, 2, 16, 128)
    recv = lax.all_to_all(packed, NAMES, split_axis=0, concat_axis=0, tiled=True)

    own_weight = head_weight.reshape(CHANS, 6 * HD)
    sib_weight = flip(head_weight, c=1).reshape(CHANS, 6 * HD)

    inner, outer = device % 16, device // 16
    gain = skip_gain.reshape(16, 2, 8, 16)[inner, :, outer]
    gain = jnp.repeat(gain.T, ROWS, axis=1)
    recv, own_weight, sib_weight, gate, at, gain = lax.optimization_barrier(
        (recv, own_weight, sib_weight, gate, at, gain)
    )
    gate = lax.all_to_all(gate, ("z", "xh", "c"), split_axis=0, concat_axis=0, tiled=True)
    filtered, gate = lax.optimization_barrier((convolve(recv, gain), gate))
    returned = lax.all_to_all(filtered, ("xl", "yh", "yl"), split_axis=0, concat_axis=0, tiled=True)
    kept, sent = apply_gate(at, returned.reshape(8, 16, 16, 128), gate)
    given = flip(sent, c=1)

    def round_z(part, way):
        near, far = along_z(part, -way), along_z(part, way)
        return {0: part, way % 4: near, -way % 4: far, 2: along_z(near, -way)}

    kept_z = round_z(kept, 1)
    given_z = [round_z(given, -1), round_z(flip(given, xh=1), 1)]
    blocks = {}
    for half, z, xh in SPOTS:
        if half == 1:
            blocks[half, z, xh] = given_z[xh][z]
        else:
            blocks[half, z, xh] = flip(kept_z[z], xh=1) if xh else kept_z[z]

    share = None
    for stage, spots in enumerate(STAGES):
        share = project(stage, at, [blocks[spot] for spot in spots], own_weight, sib_weight, share)
    mixed = collect(at, [blocks[spot] for spot in SPOTS])

    own = lax.all_to_all(share, ("xl", "yh", "yl"), split_axis=0, concat_axis=0, tiled=True)
    sib = flip(own, c=1)
    heads = attend(at, own, sib)

    out = lax.all_to_all(heads, ("xl", "yh", "yl", "z", "xh"), split_axis=0, concat_axis=0, tiled=True)
    out = out.reshape(2, 2, 2, 4, 2, PART, HD).transpose(2, 5, 3, 4, 0, 1, 6)
    return mixed, out.reshape(ROWS, CHANS)


def solution(mesh):
    fine = Mesh(mesh.devices.reshape(SIZES), NAMES)
    rows = P(NAMES, None)
    return jax.shard_map(
        per_device,
        mesh=fine,
        in_specs=(rows, rows, rows, rows, P(), P(None, ("z", "xh", "c"), None)),
        out_specs=(rows, rows),
        check_vma=False,
    )
```

```python
import functools
import itertools
import math

import jax
import jax.numpy as jnp
import ml_dtypes
import numpy as np
from jax import lax
from jax.experimental import pallas as pl
from jax.experimental.pallas import tpu as pltpu
from jax.sharding import Mesh, PartitionSpec as P

BF = jnp.bfloat16
F32 = jnp.float32
NAMES = ("xl", "yh", "yl", "z", "xh", "c")
SIZES = (2, 2, 2, 4, 2, 2)
ROWS = 64
DEVS = 128
SEQ = ROWS * DEVS
CHANS = 4096
HALF = CHANS // 2
HD = 128
VMEM_LIMIT = 60 * 1024 * 1024


def split16(table):
    table = np.asarray(table, np.float64)
    high = table.astype(np.float32).astype(ml_dtypes.bfloat16)
    low = (table - high.astype(np.float64)).astype(np.float32).astype(ml_dtypes.bfloat16)
    return high, low


def conv_tables():
    d = np.arange(DEVS)
    k1 = np.arange(DEVS) + 0.25
    r = np.arange(ROWS)
    outer = 2 * math.pi * np.outer(k1, d) / DEVS
    first = np.concatenate([np.cos(outer), -np.sin(outer)], axis=0)
    twist = 2 * math.pi * np.outer(k1, r) / SEQ
    twist_cos = np.tile(np.cos(twist), (1, 2)).astype(np.float32)
    twist_sin = np.tile(np.sin(twist), (1, 2)).astype(np.float32)
    inner = 2 * math.pi * np.outer(r, r) / ROWS
    eye = np.eye(2)
    cos, sin = np.kron(eye, np.cos(inner)), np.kron(eye, np.sin(inner))
    second = np.block([[cos, -sin], [sin, cos]])
    third = np.block([[cos, sin], [-sin, cos]])
    last = np.concatenate([np.cos(outer).T, -np.sin(outer).T], axis=1) / SEQ
    first, second, third, last = [split16(table) for table in (first, second, third, last)]
    return (
        np.concatenate(first, axis=1),
        twist_cos,
        twist_sin,
        np.concatenate([second[0], second[0], second[1]], axis=0),
        np.concatenate([third[0], third[0], third[1]], axis=0),
        np.concatenate([last[0], last[1], last[0]], axis=1),
    )


def whole(shape):
    return pl.BlockSpec(shape, lambda *_: (0,) * len(shape), memory_space=pltpu.VMEM)


def params(**more):
    return pltpu.CompilerParams(vmem_limit_bytes=VMEM_LIMIT, **more)


WIDE = CHANS // 16


def pack_kernel(key_ref, value_ref, taps_ref, gate_ref, out_ref, gate_out_ref):
    def both(ref, start):
        return jnp.concatenate(
            [ref[:, pl.ds(start + half * 128, 128)].astype(F32) for half in range(2)], axis=0
        )

    for block in range(16):
        start = block * WIDE
        product = (both(key_ref, start) * both(value_ref, start)).astype(BF).astype(F32)
        for which, tile in enumerate((product, both(taps_ref, start))):
            out_ref[:, block, which] = tile.T.astype(BF).reshape(8, 16, 128)
        gate_out_ref[block] = gate_ref[:, pl.ds(start, WIDE)]


def pack(key_signal, value_signal, long_filter, gate_signal):
    shapes = [(8, 16, 2, 16, 128), (16, ROWS, WIDE)]
    return pl.pallas_call(
        pack_kernel,
        out_shape=[jax.ShapeDtypeStruct(shape, BF) for shape in shapes],
        in_specs=[whole((ROWS, CHANS))] * 4,
        out_specs=[whole(shape) for shape in shapes],
        compiler_params=params(),
        name="pack",
    )(key_signal, value_signal, long_filter, gate_signal)


def dot(a, b):
    return jnp.dot(a, b, preferred_element_type=F32)


def cut(x):
    high = x.astype(BF)
    return high, (x - high.astype(F32)).astype(BF)


def conv_kernel(
    batch, recv_ref, gain_ref, w1, tc_ref, ts_ref, m2, m3, w3, out_ref, x_s, h_s, y_s
):
    x_s[...] = recv_ref[:, 0].astype(F32).reshape(DEVS * 16, 128)
    h_s[...] = recv_ref[:, 1].astype(F32).reshape(DEVS * 16, 128)
    tc = tc_ref[...]
    ts = ts_ref[...]

    def three(a, b):
        ah, al = cut(a)
        return dot(jnp.concatenate([ah, al, ah], axis=1), b)

    def step(it, carry):
        rows = [pl.ds(it * batch + u, DEVS, stride=16) for u in range(batch)]
        xs = [x_s[row, :] for row in rows]
        hs = [h_s[row, :] for row in rows]
        signal = jnp.concatenate([v.astype(BF) for v in xs + hs], axis=1)
        first = dot(w1[...], jnp.concatenate([signal, signal], axis=0))
        stacked = []
        for u in range(2 * batch):
            re = first[:DEVS, u * 128 : u * 128 + 128]
            im = first[DEVS:, u * 128 : u * 128 + 128]
            stacked.append(jnp.concatenate([re * tc + im * ts, im * tc - re * ts], axis=1))
        spectrum = three(jnp.concatenate(stacked, axis=0), m2[...])
        prods = []
        for u in range(batch):
            s = spectrum[u * 128 : u * 128 + 128]
            h = spectrum[(batch + u) * 128 : (batch + u) * 128 + 128]
            sr, si, hr, hi = s[:, :128], s[:, 128:], h[:, :128], h[:, 128:]
            prods.append(jnp.concatenate([sr * hr - si * hi, sr * hi + si * hr], axis=1))
        back = three(jnp.concatenate(prods, axis=0), m3[...])
        outs = []
        for u in range(batch):
            re = back[u * 128 : u * 128 + 128, :128]
            im = back[u * 128 : u * 128 + 128, 128:]
            outs.append(jnp.concatenate([re * tc - im * ts, im * tc + re * ts], axis=0))
        vh, vl = cut(jnp.concatenate(outs, axis=1))
        conv = dot(w3[...], jnp.concatenate([vh, vh, vl], axis=0))
        for u in range(batch):
            gain = gain_ref[pl.ds(it * batch + u, 1), :]
            y_s[rows[u], :] = conv[:, u * 128 : u * 128 + 128] + gain * xs[u]
        return carry

    lax.fori_loop(0, 16 // batch, step, 0)
    out_ref[...] = y_s[...].reshape(DEVS, 16, 128).astype(BF)


def convolve(recv, gain, batch=16):
    tables = conv_tables()
    args = (recv, gain, *[jnp.asarray(t) for t in tables])
    return pl.pallas_call(
        functools.partial(conv_kernel, batch),
        out_shape=jax.ShapeDtypeStruct((DEVS, 16, 128), BF),
        in_specs=[whole(a.shape) for a in args],
        out_specs=whole((DEVS, 16, 128)),
        scratch_shapes=[pltpu.VMEM((DEVS * 16, 128), F32)] * 3,
        compiler_params=params(),
        name="convolve",
    )(*args)


PART = ROWS // 2
GROUP = 8 * ROWS
ASKED = GROUP // 2
MESSAGE = 2 * GROUP + ASKED


SPOTS = [(half, z, xh) for z in range(4) for xh in range(2) for half in range(2)]
EARLY = [(0, 0, 0), (1, 0, 0), (0, 0, 1), (0, 1, 0), (0, 3, 0), (0, 2, 0), (1, 0, 1), (1, 1, 0), (1, 3, 0), (0, 1, 1)]
STAGES = [EARLY, [spot for spot in SPOTS if spot not in EARLY]]


def place(at_ref, spot):
    half, z, xh = spot
    return ((at_ref[3] + z) & 3) * 4 + (at_ref[4] ^ xh) * 2 + (at_ref[5] ^ half)


def gate_kernel(at_ref, recv_ref, gate_ref, keep_ref, send_ref):
    for side, ref in enumerate((keep_ref, send_ref)):
        for pair in range(8):
            spot = pair * 2 + (at_ref[5] ^ side)
            tile = recv_ref[:, spot].astype(F32).reshape(128, 128).T
            wide = jnp.concatenate([tile[:ROWS], tile[ROWS:]], axis=1)
            ref[pair * ROWS : pair * ROWS + ROWS] = (gate_ref[spot].astype(F32) * wide).astype(BF)


def apply_gate(at, recv, gate):
    return pl.pallas_call(
        gate_kernel,
        out_shape=[jax.ShapeDtypeStruct((GROUP, WIDE), BF)] * 2,
        in_specs=[pl.BlockSpec(memory_space=pltpu.SMEM), whole((8, 16, 16, 128)), whole((16, ROWS, WIDE))],
        out_specs=[whole((GROUP, WIDE))] * 2,
        compiler_params=params(),
        name="apply_gate",
    )(at, recv, gate)


def collect_kernel(at_ref, *refs):
    blocks, out_ref, sems = refs[:16], refs[16], refs[17]
    copies = []
    for n, block in enumerate(blocks):
        mine = pl.ds(pl.multiple_of((at_ref[3] * 2 + at_ref[4]) * ROWS, ROWS), ROWS)
        there = pl.ds(pl.multiple_of(place(at_ref, SPOTS[n]) * WIDE, WIDE), WIDE)
        copies.append(pltpu.make_async_copy(block.at[mine, :], out_ref.at[:, there], sems.at[n]))
    for copy in copies:
        copy.start()
    for copy in copies:
        copy.wait()


def collect(at, blocks):
    return pl.pallas_call(
        collect_kernel,
        out_shape=jax.ShapeDtypeStruct((ROWS, CHANS), BF),
        in_specs=[pl.BlockSpec(memory_space=pltpu.SMEM)] + [pl.BlockSpec(memory_space=pl.ANY)] * 16,
        out_specs=whole((ROWS, CHANS)),
        scratch_shapes=[pltpu.SemaphoreType.DMA((16,))],
        compiler_params=params(),
        name="collect",
    )(at, *blocks)


def project_kernel(stage, at_ref, *refs):
    spots = STAGES[stage]
    first, last = stage == 0, stage == len(STAGES) - 1
    blocks, refs = refs[: len(spots)], refs[len(spots) :]
    weights, refs = refs[:2], refs[2:]
    before, refs = (None, refs) if first else (refs[0], refs[1:])
    out_ref, x_s, w_s, acc, goal_s, load_sems, save_sems = refs
    loads = []

    def load(source, target):
        loads.append(pltpu.make_async_copy(source, target, load_sems.at[len(loads)]))
        loads[-1].start()

    for n, block in enumerate(blocks):
        load(block, x_s.at[:, pl.ds(n * WIDE, WIDE)])
    for side in range(2):
        for n, spot in enumerate(spots):
            rows = pl.ds(pl.multiple_of(place(at_ref, spot) * WIDE, WIDE), WIDE)
            load(weights[side].at[rows, :], w_s.at[side, pl.ds(n * WIDE, WIDE)])
    for side in range(0 if first else 2):
        load(before.at[side], acc.at[side])
    count = len(spots)
    for copy in loads[: len(spots)]:
        copy.wait()

    saves = []

    def save(source, target):
        saves.append(pltpu.make_async_copy(source, target, save_sems.at[len(saves)]))
        saves[-1].start()

    for side in range(2):
        for copy in loads[(side + 1) * count : (side + 2) * count]:
            copy.wait()
        done = dot(x_s[...], w_s[side])
        if not first:
            loads[3 * count + side].wait()
            done = done + acc[side]
        if not last:
            acc[side] = done
            save(acc.at[side], out_ref.at[side])
            continue
        for yh in range(2):
            start = yh * 3 * HD
            queries = done[:, start : start + HD].astype(BF).reshape(8, 2, PART, HD)
            keys = done[:, start + HD : start + 2 * HD].astype(BF)
            values = done[:, start + 2 * HD : start + 3 * HD]
            flipped = [values[n * HD : n * HD + HD].T.astype(BF) for n in range(GROUP // HD)]
            for yl in range(2):
                slot = side * 4 + yh * 2 + yl
                goal_s[slot, :GROUP] = keys
                for n, tile in enumerate(flipped):
                    goal_s[slot, GROUP + n * HD : GROUP + n * HD + HD] = tile
                goal_s[slot, 2 * GROUP :] = queries[:, yl].reshape(ASKED, HD)
                save(goal_s.at[slot], out_ref.at[(at_ref[5] ^ side) * 4 + yh * 2 + yl])
    for copy in saves:
        copy.wait()


def project(stage, at, blocks, own, sib, before=None):
    share = (2, GROUP, 6 * HD)
    message = (8, MESSAGE, HD)
    last = stage == len(STAGES) - 1
    count = len(blocks)
    return pl.pallas_call(
        functools.partial(project_kernel, stage),
        out_shape=jax.ShapeDtypeStruct(message, BF) if last else jax.ShapeDtypeStruct(share, F32),
        in_specs=[pl.BlockSpec(memory_space=pltpu.SMEM)]
        + [pl.BlockSpec(memory_space=pl.ANY)] * (count + 2 + (stage > 0)),
        out_specs=pl.BlockSpec(memory_space=pl.ANY),
        scratch_shapes=[
            pltpu.VMEM((GROUP, count * WIDE), BF),
            pltpu.VMEM((2, count * WIDE, 6 * HD), BF),
            pltpu.VMEM(share, F32),
            pltpu.VMEM(message if last else (8, 16, HD), BF),
            pltpu.SemaphoreType.DMA((3 * count + 2,)),
            pltpu.SemaphoreType.DMA((8,)),
        ],
        cost_estimate=pl.CostEstimate(
            flops=2 * GROUP * count * WIDE * 12 * HD, bytes_accessed=count * WIDE * 24 * HD, transcendentals=0
        ),
        compiler_params=params(),
        name="project_%d" % stage,
    )(at, *blocks, own, sib, *([before] if stage else []))


SCALE = math.log2(math.e) / math.sqrt(HD)
EXTRA = 16
SPAN = 2 * GROUP
KEYS = 2 * SPAN
PAIR = 2 * ASKED
ROOM = 80.0
REACH = 170.0


def attend_kernel(at_ref, *refs):
    own_hbm, sib_hbm, out_ref, k_s, v_s, q_s, acc_s, sems = refs
    my_yl, my_c = at_ref[2], at_ref[5]

    def fetch(k):
        copies = []

        def add(source, target):
            copies.append(pltpu.make_async_copy(source, target, sems.at[k, len(copies)]))

        for n in range(2):
            for side, source in enumerate((own_hbm, sib_hbm)):
                here = source.at[2 * k + n]
                first = n * SPAN + side * GROUP
                add(here.at[pl.ds(0, GROUP)], k_s.at[k, pl.ds(first, GROUP)])
                for tile in range(GROUP // HD):
                    add(
                        here.at[pl.ds(GROUP + tile * HD, HD)],
                        v_s.at[k, pl.ds(0, HD), pl.ds(first + tile * HD, HD)],
                    )
                if side == 0:
                    add(here.at[pl.ds(2 * GROUP, ASKED)], q_s.at[k, pl.ds(n * ASKED, ASKED)])
        return copies

    for k in range(4):
        for copy in fetch(k):
            copy.start()
    for k in range(4):
        v_s[k, HD:] = jnp.ones((EXTRA, KEYS), BF)

    row = lax.broadcasted_iota(jnp.int32, (KEYS, 1), 0)
    col = lax.broadcasted_iota(jnp.int32, (1, PAIR), 1)
    key_pos = (
        (row >> 10) * 1024 + ((row >> 6) & 7) * 128 + (my_c ^ ((row >> 9) & 1)) * ROWS + (row & 63)
    )
    query_pos = (col >> 8) * 1024 + ((col >> 5) & 7) * 128 + my_c * ROWS + my_yl * PART + (col & 31)

    def nt(a, b):
        return lax.dot_general(a, b, (((1,), (1,)), ((), ())), preferred_element_type=F32)

    def pair(k, tallest):
        for copy in fetch(k):
            copy.wait()
        queries = q_s[k]
        itself = jnp.concatenate(
            [
                k_s[k, pl.ds(pl.multiple_of(n * SPAN + shard * ROWS + my_yl * PART, PART), PART)]
                for n in range(2)
                for shard in range(8)
            ],
            axis=0,
        )
        ones = jnp.ones((16, HD), BF)
        square = nt(ones, jnp.square(k_s[k].astype(F32)).astype(BF))
        tallest = jnp.maximum(tallest, jnp.max(square[:8], axis=1, keepdims=True))
        size = nt(ones, jnp.square(queries.astype(F32)).astype(BF))[:1]
        bound = jnp.sqrt(size * tallest[:1]) * (SCALE * 1.02)
        product = (queries.astype(F32) * itself.astype(F32)).astype(BF)
        own = nt(ones, product)[:1] * SCALE
        safe = jnp.max(bound * 1.01 - own) <= REACH

        def score(j, masked):
            s = nt(k_s[j], queries)
            return jnp.where(key_pos <= query_pos, s, -1e30) if masked else s

        @pl.when(safe)
        def _():
            offset = bound - ROOM

            def visit(j, masked=False):
                weight = jnp.exp2(score(j, masked) * SCALE - offset).astype(BF)
                return dot(v_s[j], weight)

            acc_s[...] = visit(k, True)

            @pl.loop(0, k)
            def _(j):
                acc_s[...] += visit(j)

        @pl.when(jnp.logical_not(safe))
        def _():
            def visit(j, best, masked=False):
                s = score(j, masked)
                new = jnp.maximum(best, jnp.max(s, axis=0, keepdims=True))
                weight = jnp.exp2((s - new) * SCALE).astype(BF)
                acc_s[...] = acc_s[...] * jnp.exp2((best - new) * SCALE) + dot(v_s[j], weight)
                return new

            acc_s[...] = jnp.zeros(acc_s.shape, F32)
            best = visit(k, jnp.full((1, PAIR), -1e30, F32), True)
            lax.fori_loop(0, k, visit, best)

        out = (acc_s[:HD] / acc_s[HD : HD + 1]).T.astype(BF)
        for n in range(2):
            for shard in range(8):
                first = n * ASKED + shard * PART
                out_ref[(2 * k + n) * 8 + shard] = out[first : first + PART]
        return tallest

    lax.fori_loop(0, 4, pair, jnp.zeros((8, 1), F32))


def attend(at, own, sib):
    return pl.pallas_call(
        attend_kernel,
        out_shape=jax.ShapeDtypeStruct((64, PART, HD), BF),
        in_specs=[pl.BlockSpec(memory_space=pltpu.SMEM)] + [pl.BlockSpec(memory_space=pl.ANY)] * 2,
        out_specs=whole((64, PART, HD)),
        scratch_shapes=[
            pltpu.VMEM((4, KEYS, HD), BF),
            pltpu.VMEM((4, HD + EXTRA, KEYS), BF),
            pltpu.VMEM((4, PAIR, HD), BF),
            pltpu.VMEM((HD + EXTRA, PAIR), F32),
            pltpu.SemaphoreType.DMA((4, 22)),
        ],
        compiler_params=params(),
        name="attend",
    )(at, own, sib)


def shift(x, move):
    pairs = []
    for spot in itertools.product(*[range(n) for n in SIZES]):
        target = dict(zip(NAMES, spot))
        move(target)
        goal = [target[n] % size for n, size in zip(NAMES, SIZES)]
        pairs.append((int(np.ravel_multi_index(spot, SIZES)), int(np.ravel_multi_index(goal, SIZES))))
    return lax.ppermute(x, NAMES, pairs)


def along_z(x, step):
    def move(t):
        t["z"] = (t["z"] + step) % 4

    return shift(x, move)


def flip(x, **bits):
    def move(t):
        for name, bit in bits.items():
            t[name] ^= bit

    return shift(x, move)


def per_device(gate_signal, key_signal, value_signal, long_filter, skip_gain, head_weight):
    at = jnp.stack([lax.axis_index(name) for name in NAMES]).astype(jnp.int32)
    device = lax.axis_index(NAMES)

    packed, gate = pack(key_signal, value_signal, long_filter, gate_signal)
    packed = packed.reshape(DEVS, 2, 16, 128)
    recv = lax.all_to_all(packed, NAMES, split_axis=0, concat_axis=0, tiled=True)

    own_weight = head_weight.reshape(CHANS, 6 * HD)
    sib_weight = flip(head_weight, c=1).reshape(CHANS, 6 * HD)

    inner, outer = device % 16, device // 16
    gain = skip_gain.reshape(16, 2, 8, 16)[inner, :, outer]
    gain = jnp.repeat(gain.T, ROWS, axis=1)
    recv, own_weight, sib_weight, gate, at, gain = lax.optimization_barrier(
        (recv, own_weight, sib_weight, gate, at, gain)
    )
    gate = lax.all_to_all(gate, ("z", "xh", "c"), split_axis=0, concat_axis=0, tiled=True)
    filtered, gate = lax.optimization_barrier((convolve(recv, gain), gate))
    returned = lax.all_to_all(filtered, ("xl", "yh", "yl"), split_axis=0, concat_axis=0, tiled=True)
    kept, sent = apply_gate(at, returned.reshape(8, 16, 16, 128), gate)
    given = flip(sent, c=1)

    def round_z(part, way):
        near, far = along_z(part, -way), along_z(part, way)
        return {0: part, way % 4: near, -way % 4: far, 2: along_z(near, -way)}

    kept_z = round_z(kept, 1)
    given_z = [round_z(given, -1), round_z(flip(given, xh=1), 1)]
    blocks = {}
    for half, z, xh in SPOTS:
        if half == 1:
            blocks[half, z, xh] = given_z[xh][z]
        else:
            blocks[half, z, xh] = flip(kept_z[z], xh=1) if xh else kept_z[z]

    share = None
    for stage, spots in enumerate(STAGES):
        share = project(stage, at, [blocks[spot] for spot in spots], own_weight, sib_weight, share)
    mixed = collect(at, [blocks[spot] for spot in SPOTS])

    own = lax.all_to_all(share, ("xl", "yh", "yl"), split_axis=0, concat_axis=0, tiled=True)
    sib = flip(own, c=1)
    heads = attend(at, own, sib)

    out = lax.all_to_all(heads, ("xl", "yh", "yl", "z", "xh"), split_axis=0, concat_axis=0, tiled=True)
    out = out.reshape(2, 2, 2, 4, 2, PART, HD).transpose(2, 5, 3, 4, 0, 1, 6)
    return mixed, out.reshape(ROWS, CHANS)


def solution(mesh):
    fine = Mesh(mesh.devices.reshape(SIZES), NAMES)
    rows = P(NAMES, None)
    return jax.shard_map(
        per_device,
        mesh=fine,
        in_specs=(rows, rows, rows, rows, P(), P(None, ("z", "xh", "c"), None)),
        out_specs=(rows, rows),
        check_vma=False,
    )
```
